128 devices in a mesh: gx: 32 (over y, x_hi, z), gy: 4 (over x_lo, core).
Axes of the slice: x: 4 (x_hi: 2, x_lo: 2; x = x_hi * 2 + x_lo), y: 4, z: 4, core: 2. Of those that a mesh axis runs over, the one named last changes fastest.
Arguments:
- inputs: bfloat16 [32, 128, 32, 128], P(None, 'gx', 'gy'), may hold values from -6 to 6
- diffusion: bfloat16 [128, 32, 128], P('gx', 'gy'), may hold values from 0.049804688 to 0.5
- spectral: bfloat16 [64, 16, 2, 32, 1024], P('gx', 'gy'), may hold values from -1 to 1
- pointwise: bfloat16 [32, 32], replicated, may hold values from -1 to 1
- offsets: float32 [32], replicated, may hold values from -1 to 1
Outputs:
- activated: bfloat16 [32, 128, 32, 128], P(None, 'gx', 'gy')
The draws below stay inside these ranges and needn't reach their ends.
All inputs are finite; a program needn't handle non-finite values.
Results may differ from the reference program's by a relative error of at most 0.006.
Values may be sent and summed in bfloat16 or wider, within the bound.
A program may use at most 64 MiB of HBM per device.

```python
import math
import jax
import jax.numpy as jnp
from jax import lax

C = 32
MY = 16
MZ = 32
NZ = 128
MX = 64
NX = 128
NY = 32


def block_scale(own_key, shape, split, low, top_value):
    def one(position, shards_of):
        heights = jax.random.uniform(jax.random.fold_in(jax.random.fold_in(own_key, 6), position), (shards_of,), jnp.float32, low / len(split), top_value / len(split))
        return jnp.repeat(jnp.exp(heights), shape[position] // shards_of).reshape((-1,) + (1,) * (len(shape) - position - 1))

    loudness = one(*split[0])
    for cut in split[1:]:
        loudness = loudness * one(*cut)
    return loudness


def normal_values(rng, dims, scale, most, shards=(), kind=jnp.bfloat16):
    drawn = jax.random.normal(rng, dims, jnp.float32) * scale
    if len(shards) > 0:
        drawn = block_scale(rng, dims, shards, -0.22, 0.18) * drawn
    return jnp.clip(drawn, min=-most, max=most).astype(kind)


def setup_inputs(seed: int = 0) -> dict:
    seeds = jax.random.split(jax.random.key(seed), 6)
    return {
        "inputs": normal_values(seeds[0], (C, NX, NY, NZ), 1.0, 6.0, ((1, 32), (2, 4))),
        "diffusion": jnp.clip(jnp.exp(math.log(0.5) - 2.306499 * jax.random.uniform(seeds[1], (NX, NY, NZ), jnp.float32) ** block_scale(seeds[1], (NX, NY, NZ), ((0, 32), (1, 4)), -0.2, 0.2)), 0.049804688, 0.5).astype(jnp.bfloat16),
        "spectral": normal_values(seeds[2], (MX, MY, 2, C, C * MZ), C ** -0.5, 1.0, ((0, 32), (1, 4))),
        "pointwise": normal_values(seeds[3], (C, C), C ** -0.5, 1.0),
        "offsets": jnp.clip(jax.random.uniform(seeds[4], (C,), jnp.float32, -1.0, 1.0), -1.0, 1.0),
    }


def frequencies(modes):
    indices = jnp.arange(modes, dtype=jnp.int32)
    return jnp.where(indices < modes // 2, indices, indices - modes).astype(jnp.int32)

def phase_table(positions, waves, length, rotate):
    windings = positions[:, None] * waves[None, :] % length
    angles = 2.0 * math.pi / length * windings.astype(jnp.float32)
    cosine = jnp.cos(angles)
    sines = rotate * jnp.sin(angles)
    from_real = jnp.stack([cosine, sines], axis=-1)
    from_imag = jnp.stack([-sines, cosine], axis=-1)
    return jnp.stack([from_real, from_imag], axis=1)

def z_tables(length_z, modes_z):
    positions = jnp.arange(length_z, dtype=jnp.int32)
    waves = jnp.arange(modes_z, dtype=jnp.int32)
    forward = phase_table(positions, waves, length_z, -1.0)[:, 0, :, :]
    forward = jnp.transpose(forward, (0, 2, 1)).reshape(length_z, 2 * modes_z)
    backward = phase_table(positions, waves, length_z, 1.0)[:, :, :, 0]
    backward = jnp.transpose(backward, (1, 2, 0)).reshape(2 * modes_z, length_z)
    return (forward.astype(jnp.bfloat16), backward)

def contract(u_part, w_part):
    return jnp.einsum('cakz,akcoz->oakz', u_part, w_part, precision=lax.Precision.HIGHEST)

def reference(inputs, diffusion, spectral, pointwise, offsets):
    highest = lax.Precision.HIGHEST
    z_forward, z_inverse = z_tables(NZ, MZ)
    z_spectrum = jnp.dot(inputs.reshape(-1, NZ), z_forward, preferred_element_type=jnp.float32)
    z_spectrum = z_spectrum.reshape(C, NX, NY, 2, MZ)
    y_table = phase_table(jnp.arange(NY, dtype=jnp.int32), frequencies(MY), NY, -1.0)
    y_partial = jnp.einsum('cxyqz,yqkp->cxkpz', z_spectrum, y_table, precision=highest)
    x_table = phase_table(jnp.arange(NX, dtype=jnp.int32), frequencies(MX), NX, -1.0)
    modes = jnp.einsum('cxkqz,xqap->cakpz', y_partial, x_table, precision=highest)
    modes = modes * (1.0 / math.sqrt(NX * NY * NZ))
    weights = spectral.astype(jnp.float32).reshape(MX, MY, 2, C, C, MZ)
    w_real = weights[:, :, 0]
    w_imag = weights[:, :, 1]
    u_real = modes[:, :, :, 0]
    u_imag = modes[:, :, :, 1]
    y_real = contract(u_real, w_real) - contract(u_imag, w_imag)
    y_imag = contract(u_real, w_imag) + contract(u_imag, w_real)
    mixed = jnp.stack([y_real, y_imag], axis=3).astype(jnp.bfloat16)
    x_inverse = jnp.transpose(phase_table(jnp.arange(NX, dtype=jnp.int32), frequencies(MX), NX, 1.0), (2, 1, 0, 3))
    y_inverse = jnp.transpose(phase_table(jnp.arange(NY, dtype=jnp.int32), frequencies(MY), NY, 1.0), (2, 1, 0, 3))
    back_x = jnp.einsum('oakqz,aqxp->oxkpz', mixed.astype(jnp.float32), x_inverse, precision=highest)
    spatial = jnp.einsum('oxkqz,kqyp->oxypz', back_x, y_inverse, precision=highest)
    inverse_scale = 1.0 / math.sqrt(MX * MY * MZ)

    def x_slice(index_x):
        local_modes = lax.dynamic_slice_in_dim(spatial, index_x, 1, 1).reshape(-1, 2 * MZ)
        spectral_out = jnp.dot(local_modes, z_inverse, precision=highest, preferred_element_type=jnp.float32)
        spectral_out = spectral_out.reshape(C, NY, NZ) * inverse_scale
        values = lax.dynamic_slice_in_dim(inputs, index_x, 1, 1).reshape(C, NY, NZ)
        mixing = jnp.dot(pointwise, values.reshape(C, -1), preferred_element_type=jnp.float32).reshape(C, NY, NZ)
        widened = values.astype(jnp.float32)
        padded = jnp.pad(widened, ((0, 0), (0, 0), (1, 1)))
        curvature = padded[:, :, 2:] - 2.0 * widened + padded[:, :, :-2]
        local_coeff = lax.dynamic_slice_in_dim(diffusion, index_x, 1, 0).reshape(NY, NZ).astype(jnp.float32)
        summed_all = spectral_out + mixing + local_coeff[None] * curvature + offsets[:, None, None]
        return jax.nn.gelu(summed_all, approximate=False).astype(jnp.bfloat16)
    slices = lax.map(x_slice, jnp.arange(NX, dtype=jnp.int32))
    return jnp.transpose(slices, (1, 0, 2, 3))
```

```python
import functools

import jax
import jax.numpy as jnp
import numpy as np
from jax import lax
from jax.experimental import pallas as pl
from jax.experimental.pallas import tpu as pltpu
from jax.sharding import PartitionSpec as P

MESH = pl.DeviceIdType.MESH
BF = jnp.bfloat16
F32 = jnp.float32

NT = (((1,), (1,)), ((), ()))
TN = (((0,), (0,)), ((), ()))
NN = (((1,), (0,)), ((), ()))


def mm(a, b, dims=NN):
    return lax.dot_general(a, b, dims, preferred_element_type=F32)


def freq(n):
    j = np.arange(n)
    return np.where(j < n // 2, j, j - n)


def turn(a, b, n):
    return 2.0 * np.pi / n * ((a * b) % n)


def parts(z):
    return np.stack([z.real, z.imag])


def tables():
    eye4, eye8 = np.eye(4), np.eye(8)
    z, kz = np.arange(128), np.arange(32)
    a = parts(np.exp(-1j * turn(kz[:, None], z[None, :], 128)))
    tz = np.einsum("rkz,xw->rkxwz", a, eye4).reshape(256, 512)
    x = 4 * (4 * np.arange(8)[None, :, None] + np.arange(4)[:, None, None]) + np.arange(4)
    kx = freq(64).reshape(32, 2).T
    th = turn(kx[None, None, None, :, :], x[:, :, :, None, None], 128)
    cs = np.stack([np.cos(th), np.sin(th)])
    tx = np.einsum("sZYxlg,cd->ZslgcYdx", cs, eye4).reshape(4, 512, 128)
    y = np.arange(32).reshape(4, 8)
    ky = freq(16).reshape(4, 4)
    ph = turn(y[:, :, None, None], ky[None, None], 32)
    unit = np.array([1.0, 1j])
    co = np.einsum("hyHk,s,r->hyHksr", np.exp(-1j * ph), np.conj(unit), unit)
    ty = np.einsum("qhyHksr,cd->shrcyHkqd", parts(co), eye8).reshape(1024, 256)
    txi = np.einsum("sZYxlg,cd->ZsYcxlgd", cs, eye4).reshape(4, 256, 256)
    co = np.einsum("HyhK,s,r->HyhKsr", np.exp(1j * ph), unit, unit)
    tyi = np.einsum("qHyhKsr,bd->shbKrHqdy", parts(co), eye8).reshape(512, 512)
    b = np.exp(1j * turn(kz[:, None], z[None, :], 128)) * 2.0**-7.5
    tzi = np.einsum("rkz,xw->rkxwz", np.stack([b.real, -b.imag]), eye4).reshape(256, 512)
    return [jnp.asarray(np.asarray(t, np.float32)).astype(BF) for t in (tz, tx, ty, txi, tyi, tzi)]


def iota(shape, dim):
    return lax.broadcasted_iota(jnp.int32, shape, dim)


def one_hot(cond):
    return jnp.where(cond, 1.0, 0.0).astype(BF)


def cells_by_x(x):
    wide = x.astype(F32).reshape(32, 4, 8, 128)
    return jnp.concatenate([wide[:, k].reshape(256, 128) for k in range(4)], axis=1)


def forward_z(xx, tz):
    out = mm(tz, xx, NT)
    res = []
    for q in range(4):
        lanes = slice(q * 64, q * 64 + 64)
        both = jnp.concatenate([out[:128, lanes], out[128:, lanes]], axis=1)
        res.append(both.astype(BF).reshape(32, 4, 128))
    return res


def before_gelu(wide, xx, diff, point, offset):
    rep = one_hot(iota((256, 32), 0) // 8 == iota((256, 32), 1))
    spread = mm(mm(rep, point).astype(BF), rep, NT)
    same_y = iota((256, 256), 0) % 8 == iota((256, 256), 1) % 8
    kron = jnp.where(same_y, spread, 0.0).astype(BF)
    mix = mm(kron, xx)
    gap = iota((128, 128), 0) - iota((128, 128), 1)
    sten = jnp.where(gap == 0, -2.0, jnp.where((gap == 1) | (gap == -1), 1.0, 0.0)).astype(BF)
    cols = []
    for k in range(4):
        lanes = slice(k * 128, k * 128 + 128)
        curv = mm(xx[:, lanes], sten).reshape(32, 8, 128)
        cols.append((curv * diff[k][None]).reshape(256, 128))
    shift = jnp.concatenate([jnp.full((8, 512), offset(o), F32) for o in range(32)], axis=0)
    return mix + jnp.concatenate(cols, axis=1) + shift


def forward_xy(r1, tx, ty):
    r1 = r1.reshape(512, 128)
    d = jnp.concatenate([r1[h * 128 : h * 128 + 128] for h in range(4)], axis=1)
    g = mm(tx, d).astype(BF)
    g = jnp.concatenate([g[:256], g[256:]], axis=1)
    o = mm(g, ty)
    res = []
    for h in range(4):
        lanes = slice(h * 64, h * 64 + 64)
        both = jnp.concatenate([o[:128, lanes], o[128:, lanes]], axis=1)
        res.append(both.astype(BF).reshape(32, 4, 128))
    return res


def own_modes(r2):
    r2 = r2.reshape(512, 128).astype(F32)
    u = r2[:128] + r2[128:256] + r2[256:384] + r2[384:]
    hi = u.astype(BF)
    lo = (u - hi.astype(F32)).astype(BF)
    row, col = iota((256, 512), 0), iota((256, 512), 1)
    row = row % 128
    rep = one_hot((row % 4 == col // 128) & (row // 4 == col % 32))
    return mm(jnp.concatenate([hi, lo], axis=0), rep, TN) * (2.0**-9.5)


def mix_modes(u, w):
    rows = []
    for j in range(8):
        wr, wi = w(2 * j).astype(F32), w(2 * j + 1).astype(F32)
        re = im = None
        for q in range(4):
            ur = jnp.concatenate([u[16 * j : 16 * j + 8, q * 128 : q * 128 + 128]] * 8, axis=1)
            ui = jnp.concatenate([u[16 * j + 8 : 16 * j + 16, q * 128 : q * 128 + 128]] * 8, axis=1)
            r, i = wr[q * 8 : q * 8 + 8], wi[q * 8 : q * 8 + 8]
            a, b = r * ur - i * ui, r * ui + i * ur
            re, im = (a, b) if re is None else (re + a, im + b)
        rows += [jnp.sum(re, axis=0, keepdims=True), jnp.sum(im, axis=0, keepdims=True)]
    y = jnp.concatenate(rows, axis=0)
    a = jnp.concatenate(
        [y[l * 8 : l * 8 + 8, b * 128 : b * 128 + 128] for l in range(2) for b in range(8)], axis=0
    ).astype(BF)
    row, col = iota((128, 128), 0), iota((128, 128), 1)
    perm = one_hot((row % 4 == col // 32) & (row // 4 == col % 32))
    return mm(perm, a, NT).astype(BF).reshape(32, 4, 128)


def inverse_xy(r3, txi, tyi):
    r3 = r3.reshape(512, 128)
    d = jnp.concatenate(
        [
            jnp.concatenate([r3[h * 128 : h * 128 + 128, l * 64 : l * 64 + 64] for h in range(4)], axis=1)
            for l in range(2)
        ],
        axis=0,
    )
    g = mm(txi, d).astype(BF)
    o = mm(jnp.concatenate([g[:128], g[128:]], axis=1), tyi).astype(BF)
    return [o[:, h * 128 : h * 128 + 128].reshape(8, 4, 4, 128) for h in range(4)]


def inverse_z(r4, tzi):
    halves = [
        jnp.concatenate([r4[o].reshape(128, 128)[:, r * 64 : r * 64 + 64] for o in range(4)], axis=1)
        for r in range(2)
    ]
    res = mm(jnp.concatenate(halves, axis=0), tzi, TN)
    return jnp.transpose(res.reshape(4, 8, 8, 512), (1, 0, 2, 3)).reshape(256, 512)


def gelu(v):
    return 0.5 * v * (1.0 + lax.erf(v * (0.5**0.5)))


def far_first(sizes):
    steps = [()]
    for n in sizes:
        steps = [s + (k,) for s in steps for k in range(n)]
    steps = [s + (c,) for s in steps for c in range(2)]
    steps.sort(key=lambda s: (-sum(min(k, n - k) for k, n in zip(s, sizes)), -s[-1]))
    return steps[:-1]


def kernel(
    x_hbm, diff_hbm, w_hbm, point_ref, off_ref, tz_hbm, tx_hbm, ty_hbm, txi_hbm, tyi_hbm, tzi_hbm,
    out_ref,
    x_v, diff_v, w_v, tz_v, tx_v, ty_v, txi_v, tyi_v, tzi_v, pre_v,
    s1, r1, s2, r2, s3, r3, s4, r4, load_sem, send_sem, recv_sem,
):
    g, h = lax.axis_index("gx"), lax.axis_index("gy")
    plane, zz = g // 4, g % 4
    kz = plane * 4 + h
    yy, xc, core = g // 8, (plane % 2) * 2 + h // 2, h % 2
    ys = [lax.rem(yy + k, 4) * 8 for k in range(4)]
    zs = [lax.rem(zz + k, 4) for k in range(4)]
    xs = [lax.rem(xc + k, 4) for k in range(4)]
    ups = [[ys[a] + xs[b] // 2 * 4 for b in range(4)] for a in range(4)]
    gys = [[xs[b] % 2 * 2 + c for c in (core, 1 - core)] for b in range(4)]
    everyone = [(ups[a][b] + zs[c], gys[b][d]) for a, b, c, d in far_first((4, 4, 4))]
    planar = [(ups[a][b], gys[b][d]) for a, b, d in far_first((4, 4))]

    barrier = pltpu.get_barrier_semaphore()
    for peer in everyone:
        pl.semaphore_signal(barrier, inc=1, device_id=peer, device_id_type=MESH)

    loads = [
        (x_hbm, x_v), (tz_hbm, tz_v), (diff_hbm, diff_v), (tx_hbm.at[zz], tx_v), (ty_hbm, ty_v),
        (w_hbm, w_v), (txi_hbm.at[zz], txi_v), (tyi_hbm, tyi_v), (tzi_hbm, tzi_v),
    ]
    loads = [pltpu.make_async_copy(a, b, load_sem.at[k]) for k, (a, b) in enumerate(loads)]
    for c in loads:
        c.start()
    loads[0].wait()
    loads[1].wait()
    xx = cells_by_x(x_v[...]).astype(BF)
    for q, block in enumerate(forward_z(xx, tz_v[...])):
        s1[:, q] = block
    loads[2].wait()
    diff = diff_v[...].astype(F32)
    pre_v[...] = before_gelu(None, xx, diff, point_ref[...], lambda o: off_ref[o])
    for c in loads[3:]:
        c.wait()
    pl.semaphore_wait(barrier, 127)

    def send(src, dst, phase, peer):
        pltpu.make_async_remote_copy(
            src, dst, send_sem.at[phase], recv_sem.at[phase], device_id=peer, device_id_type=MESH
        ).start()

    def wait(ref, sem):
        pltpu.make_async_copy(ref, ref, sem).wait()

    slot = h * 8 + plane
    for up, gy in planar:
        send(s1.at[up + gy], r1.at[slot], 0, (up + zz, gy))
    r1[slot] = s1[kz]
    wait(r1.at[pl.ds(0, 31)], recv_sem.at[0])

    for k, block in enumerate(forward_xy(r1[...], tx_v[...], ty_v[...])):
        s2[k] = block
    slot = zz * 32 + kz
    for gx, gy in everyone:
        send(s2.at[gy, gx], r2.at[slot], 1, (gx, gy))
    r2[slot] = s2[h, g]
    wait(r2.at[pl.ds(0, 127)], recv_sem.at[1])

    s3[...] = mix_modes(own_modes(r2[...]), lambda m: w_v[m])
    slot = h * 32 + g
    for a, b, c, d in far_first((4, 4, 4)):
        up, gy = ups[a][b], gys[b][d]
        send(s3.at[up + gy], r3.at[slot], 2, (up + zs[c], gy))
    r3[slot] = s3[kz]
    wait(r3.at[pl.ds(0, 127)], recv_sem.at[2])

    for k, block in enumerate(inverse_xy(r3[...], txi_v[...], tyi_v[...])):
        s4[:, k] = block
    for up, gy in planar:
        send(s4.at[up // 4, gy], r4.at[:, kz], 3, (up + zz, gy))
    r4[:, kz] = s4[plane, h]
    wait(r1.at[pl.ds(0, 31)], recv_sem.at[3])

    act = gelu(pre_v[...] + inverse_z(r4[...], tzi_v[...]))
    act = jnp.stack([act[:, k * 128 : k * 128 + 128].reshape(32, 8, 128) for k in range(4)], axis=1)
    out_ref[...] = act.reshape(1024, 128).astype(BF)

    wait(s1.at[pl.ds(0, 31)], send_sem.at[0])
    wait(r2.at[pl.ds(0, 127)], send_sem.at[1])
    wait(r2.at[pl.ds(0, 127)], send_sem.at[2])
    wait(s1.at[pl.ds(0, 31)], send_sem.at[3])


def on_device(inputs, diffusion, spectral, pointwise, offsets):
    hbm = pl.BlockSpec(memory_space=pl.ANY)
    vmem = pl.BlockSpec(memory_space=pltpu.VMEM)
    smem = pl.BlockSpec(memory_space=pltpu.SMEM)
    v = pltpu.VMEM
    out = pl.pallas_call(
        kernel,
        out_shape=jax.ShapeDtypeStruct((1024, 128), BF),
        in_specs=[hbm, hbm, hbm, vmem, smem] + [hbm] * 6,
        out_specs=vmem,
        scratch_shapes=[
            v((1024, 128), BF), v((4, 8, 128), BF), v((16, 32, 1024), BF),
            v((256, 512), BF), v((512, 128), BF), v((1024, 256), BF),
            v((256, 256), BF), v((512, 512), BF), v((256, 512), BF), v((256, 512), F32),
            v((32, 4, 4, 128), BF), v((32, 4, 4, 128), BF),
            v((4, 32, 4, 128), BF), v((128, 4, 128), BF),
            v((32, 4, 128), BF), v((128, 4, 128), BF),
            v((8, 4, 4, 4, 128), BF), v((4, 32, 4, 128), BF),
            pltpu.SemaphoreType.DMA((9,)), pltpu.SemaphoreType.DMA((4,)), pltpu.SemaphoreType.DMA((4,)),
        ],
        compiler_params=pltpu.CompilerParams(
            collective_id=0, has_side_effects=True, vmem_limit_bytes=50 << 20
        ),
    )(
        inputs.reshape(1024, 128),
        diffusion,
        spectral.reshape(16, 32, 1024),
        pointwise,
        offsets,
        *tables(),
    )
    return out.reshape(32, 4, 8, 128)


def solution(mesh):
    return jax.shard_map(
        on_device,
        mesh=mesh,
        in_specs=(P(None, "gx", "gy", None), P("gx", "gy", None), P("gx", "gy", None, None, None), P(), P()),
        out_specs=P(None, "gx", "gy", None),
        check_vma=False,
    )
```

```python
import functools

import jax
import jax.numpy as jnp
import numpy as np
from jax import lax
from jax.experimental import pallas as pl
from jax.experimental.pallas import tpu as pltpu
from jax.sharding import PartitionSpec as P

MESH = pl.DeviceIdType.MESH
BF = jnp.bfloat16
F32 = jnp.float32

NT = (((1,), (1,)), ((), ()))
TN = (((0,), (0,)), ((), ()))
NN = (((1,), (0,)), ((), ()))


def mm(a, b, dims=NN):
    return lax.dot_general(a, b, dims, preferred_element_type=F32)


def freq(n):
    j = np.arange(n)
    return np.where(j < n // 2, j, j - n)


def turn(a, b, n):
    return 2.0 * np.pi / n * ((a * b) % n)


def parts(z):
    return np.stack([z.real, z.imag])


def tables():
    eye4, eye8 = np.eye(4), np.eye(8)
    z, kz = np.arange(128), np.arange(32)
    a = parts(np.exp(-1j * turn(kz[:, None], z[None, :], 128)))
    tz = np.einsum("rkz,xw->rkxwz", a, eye4).reshape(256, 512)
    x = 4 * (4 * np.arange(8)[None, :, None] + np.arange(4)[:, None, None]) + np.arange(4)
    kx = freq(64).reshape(32, 2).T
    th = turn(kx[None, None, None, :, :], x[:, :, :, None, None], 128)
    cs = np.stack([np.cos(th), np.sin(th)])
    tx = np.einsum("sZYxlg,cd->ZslgcYdx", cs, eye4).reshape(4, 512, 128)
    y = np.arange(32).reshape(4, 8)
    ky = freq(16).reshape(4, 4)
    ph = turn(y[:, :, None, None], ky[None, None], 32)
    unit = np.array([1.0, 1j])
    co = np.einsum("hyHk,s,r->hyHksr", np.exp(-1j * ph), np.conj(unit), unit)
    ty = np.einsum("qhyHksr,cd->shrcyHkqd", parts(co), eye8).reshape(1024, 256)
    txi = np.einsum("sZYxlg,cd->ZsYcxlgd", cs, eye4).reshape(4, 256, 256)
    co = np.einsum("HyhK,s,r->HyhKsr", np.exp(1j * ph), unit, unit)
    tyi = np.einsum("qHyhKsr,bd->shbKrHqdy", parts(co), eye8).reshape(512, 512)
    b = np.exp(1j * turn(kz[:, None], z[None, :], 128)) * 2.0**-7.5
    tzi = np.einsum("rkz,xw->rkxwz", np.stack([b.real, -b.imag]), eye4).reshape(256, 512)
    return [jnp.asarray(np.asarray(t, np.float32)).astype(BF) for t in (tz, tx, ty, txi, tyi, tzi)]


def iota(shape, dim):
    return lax.broadcasted_iota(jnp.int32, shape, dim)


def one_hot(cond):
    return jnp.where(cond, 1.0, 0.0).astype(BF)


def cells_by_x(x):
    wide = x.astype(F32).reshape(32, 4, 8, 128)
    return jnp.concatenate([wide[:, k].reshape(256, 128) for k in range(4)], axis=1)


def forward_z(xx, tz):
    out = mm(tz, xx, NT)
    res = []
    for q in range(4):
        lanes = slice(q * 64, q * 64 + 64)
        both = jnp.concatenate([out[:128, lanes], out[128:, lanes]], axis=1)
        res.append(both.astype(BF).reshape(32, 4, 128))
    return res


def before_gelu(wide, xx, diff, point, offset):
    rep = one_hot(iota((256, 32), 0) // 8 == iota((256, 32), 1))
    spread = mm(mm(rep, point).astype(BF), rep, NT)
    same_y = iota((256, 256), 0) % 8 == iota((256, 256), 1) % 8
    kron = jnp.where(same_y, spread, 0.0).astype(BF)
    mix = mm(kron, xx)
    gap = iota((128, 128), 0) - iota((128, 128), 1)
    sten = jnp.where(gap == 0, -2.0, jnp.where((gap == 1) | (gap == -1), 1.0, 0.0)).astype(BF)
    cols = []
    for k in range(4):
        lanes = slice(k * 128, k * 128 + 128)
        curv = mm(xx[:, lanes], sten).reshape(32, 8, 128)
        cols.append((curv * diff[k][None]).reshape(256, 128))
    shift = jnp.concatenate([jnp.full((8, 512), offset(o), F32) for o in range(32)], axis=0)
    return mix + jnp.concatenate(cols, axis=1) + shift


def forward_xy(r1, tx, ty):
    r1 = r1.reshape(512, 128)
    d = jnp.concatenate([r1[h * 128 : h * 128 + 128] for h in range(4)], axis=1)
    g = mm(tx, d).astype(BF)
    g = jnp.concatenate([g[:256], g[256:]], axis=1)
    o = mm(g, ty)
    res = []
    for h in range(4):
        lanes = slice(h * 64, h * 64 + 64)
        both = jnp.concatenate([o[:128, lanes], o[128:, lanes]], axis=1)
        res.append(both.astype(BF).reshape(32, 4, 128))
    return res


def own_modes(r2):
    r2 = r2.reshape(512, 128).astype(F32)
    u = r2[:128] + r2[128:256] + r2[256:384] + r2[384:]
    hi = u.astype(BF)
    lo = (u - hi.astype(F32)).astype(BF)
    row, col = iota((256, 512), 0), iota((256, 512), 1)
    row = row % 128
    rep = one_hot((row % 4 == col // 128) & (row // 4 == col % 32))
    return mm(jnp.concatenate([hi, lo], axis=0), rep, TN) * (2.0**-9.5)


def mix_modes(u, w):
    rows = []
    for j in range(8):
        wr, wi = w(2 * j).astype(F32), w(2 * j + 1).astype(F32)
        re = im = None
        for q in range(4):
            ur = jnp.concatenate([u[16 * j : 16 * j + 8, q * 128 : q * 128 + 128]] * 8, axis=1)
            ui = jnp.concatenate([u[16 * j + 8 : 16 * j + 16, q * 128 : q * 128 + 128]] * 8, axis=1)
            r, i = wr[q * 8 : q * 8 + 8], wi[q * 8 : q * 8 + 8]
            a, b = r * ur - i * ui, r * ui + i * ur
            re, im = (a, b) if re is None else (re + a, im + b)
        rows += [jnp.sum(re, axis=0, keepdims=True), jnp.sum(im, axis=0, keepdims=True)]
    y = jnp.concatenate(rows, axis=0)
    a = jnp.concatenate(
        [y[l * 8 : l * 8 + 8, b * 128 : b * 128 + 128] for l in range(2) for b in range(8)], axis=0
    ).astype(BF)
    row, col = iota((128, 128), 0), iota((128, 128), 1)
    perm = one_hot((row % 4 == col // 32) & (row // 4 == col % 32))
    return mm(perm, a, NT).astype(BF).reshape(32, 4, 128)


def inverse_xy(r3, txi, tyi):
    r3 = r3.reshape(512, 128)
    d = jnp.concatenate(
        [
            jnp.concatenate([r3[h * 128 : h * 128 + 128, l * 64 : l * 64 + 64] for h in range(4)], axis=1)
            for l in range(2)
        ],
        axis=0,
    )
    g = mm(txi, d).astype(BF)
    o = mm(jnp.concatenate([g[:128], g[128:]], axis=1), tyi).astype(BF)
    return [o[:, h * 128 : h * 128 + 128].reshape(8, 4, 4, 128) for h in range(4)]


def inverse_z(r4, tzi):
    halves = [
        jnp.concatenate([r4[o].reshape(128, 128)[:, r * 64 : r * 64 + 64] for o in range(4)], axis=1)
        for r in range(2)
    ]
    res = mm(jnp.concatenate(halves, axis=0), tzi, TN)
    return jnp.transpose(res.reshape(4, 8, 8, 512), (1, 0, 2, 3)).reshape(256, 512)


def gelu(v):
    return 0.5 * v * (1.0 + lax.erf(v * (0.5**0.5)))


def far_first(sizes):
    steps = [()]
    for n in sizes:
        steps = [s + (k,) for s in steps for k in range(n)]
    steps = [s + (c,) for s in steps for c in range(2)]
    steps.sort(key=lambda s: (-sum(min(k, n - k) for k, n in zip(s, sizes)), -s[-1]))
    return steps[:-1]


def kernel(
    x_hbm, diff_hbm, w_hbm, point_hbm, off_hbm, tz_hbm, tx_hbm, ty_hbm, txi_hbm, tyi_hbm, tzi_hbm,
    out_ref,
    x_v, diff_v, w_v, point_ref, off_ref, tz_v, tx_v, ty_v, txi_v, tyi_v, tzi_v, pre_v,
    s1, r1, s2, r2, s3, r3, s4, r4, load_sem, send_sem, recv_sem,
):
    g, h = lax.axis_index("gx"), lax.axis_index("gy")
    plane, zz = g // 4, g % 4
    kz = plane * 4 + h
    yy, xc, core = g // 8, (plane % 2) * 2 + h // 2, h % 2
    ys = [lax.rem(yy + k, 4) * 8 for k in range(4)]
    zs = [lax.rem(zz + k, 4) for k in range(4)]
    xs = [lax.rem(xc + k, 4) for k in range(4)]
    ups = [[ys[a] + xs[b] // 2 * 4 for b in range(4)] for a in range(4)]
    gys = [[xs[b] % 2 * 2 + c for c in (core, 1 - core)] for b in range(4)]
    everyone = [(ups[a][b] + zs[c], gys[b][d]) for a, b, c, d in far_first((4, 4, 4))]
    planar = [(ups[a][b], gys[b][d]) for a, b, d in far_first((4, 4))]

    barrier = pltpu.get_barrier_semaphore()
    for peer in everyone:
        pl.semaphore_signal(barrier, inc=1, device_id=peer, device_id_type=MESH)

    loads = [
        (x_hbm, x_v), (tz_hbm, tz_v), (diff_hbm, diff_v), (point_hbm, point_ref), (off_hbm, off_ref), (tx_hbm.at[zz], tx_v), (ty_hbm, ty_v),
        (w_hbm, w_v), (txi_hbm.at[zz], txi_v), (tyi_hbm, tyi_v), (tzi_hbm, tzi_v),
    ]
    loads = [pltpu.make_async_copy(a, b, load_sem.at[k]) for k, (a, b) in enumerate(loads)]
    for c in loads:
        c.start()
    loads[0].wait()
    loads[1].wait()
    xx = cells_by_x(x_v[...]).astype(BF)
    for q, block in enumerate(forward_z(xx, tz_v[...])):
        s1[:, q] = block
    for c in loads[2:5]:
        c.wait()
    diff = diff_v[...].astype(F32)
    pre_v[...] = before_gelu(None, xx, diff, point_ref[...], lambda o: off_ref[o])
    for c in loads[5:]:
        c.wait()
    pl.semaphore_wait(barrier, 127)

    def send(src, dst, phase, peer):
        pltpu.make_async_remote_copy(
            src, dst, send_sem.at[phase], recv_sem.at[phase], device_id=peer, device_id_type=MESH
        ).start()

    def wait(ref, sem):
        pltpu.make_async_copy(ref, ref, sem).wait()

    slot = h * 8 + plane
    for up, gy in planar:
        send(s1.at[up + gy], r1.at[slot], 0, (up + zz, gy))
    r1[slot] = s1[kz]
    wait(r1.at[pl.ds(0, 31)], recv_sem.at[0])

    for k, block in enumerate(forward_xy(r1[...], tx_v[...], ty_v[...])):
        s2[k] = block
    slot = zz * 32 + kz
    for gx, gy in everyone:
        send(s2.at[gy, gx], r2.at[slot], 1, (gx, gy))
    r2[slot] = s2[h, g]
    wait(r2.at[pl.ds(0, 127)], recv_sem.at[1])

    s3[...] = mix_modes(own_modes(r2[...]), lambda m: w_v[m])
    slot = h * 32 + g
    for a, b, c, d in far_first((4, 4, 4)):
        up, gy = ups[a][b], gys[b][d]
        send(s3.at[up + gy], r3.at[slot], 2, (up + zs[c], gy))
    r3[slot] = s3[kz]
    wait(r3.at[pl.ds(0, 127)], recv_sem.at[2])

    for k, block in enumerate(inverse_xy(r3[...], txi_v[...], tyi_v[...])):
        s4[:, k] = block
    for up, gy in planar:
        send(s4.at[up // 4, gy], r4.at[:, kz], 3, (up + zz, gy))
    r4[:, kz] = s4[plane, h]
    wait(r1.at[pl.ds(0, 31)], recv_sem.at[3])

    act = gelu(pre_v[...] + inverse_z(r4[...], tzi_v[...]))
    act = jnp.stack([act[:, k * 128 : k * 128 + 128].reshape(32, 8, 128) for k in range(4)], axis=1)
    out_ref[...] = act.reshape(1024, 128).astype(BF)

    wait(s1.at[pl.ds(0, 31)], send_sem.at[0])
    wait(r2.at[pl.ds(0, 127)], send_sem.at[1])
    wait(r2.at[pl.ds(0, 127)], send_sem.at[2])
    wait(s1.at[pl.ds(0, 31)], send_sem.at[3])


def on_device(inputs, diffusion, spectral, pointwise, offsets):
    hbm = pl.BlockSpec(memory_space=pltpu.HBM)
    vmem = pl.BlockSpec(memory_space=pltpu.VMEM)
    v = pltpu.VMEM
    out = pl.pallas_call(
        kernel,
        out_shape=jax.ShapeDtypeStruct((1024, 128), BF),
        in_specs=[hbm] * 11,
        out_specs=vmem,
        scratch_shapes=[
            v((1024, 128), BF), v((4, 8, 128), BF), v((16, 32, 1024), BF), v((32, 32), BF), pltpu.SMEM((32,), F32),
            v((256, 512), BF), v((512, 128), BF), v((1024, 256), BF),
            v((256, 256), BF), v((512, 512), BF), v((256, 512), BF), v((256, 512), F32),
            v((32, 4, 4, 128), BF), v((32, 4, 4, 128), BF),
            v((4, 32, 4, 128), BF), v((128, 4, 128), BF),
            v((32, 4, 128), BF), v((128, 4, 128), BF),
            v((8, 4, 4, 4, 128), BF), v((4, 32, 4, 128), BF),
            pltpu.SemaphoreType.DMA((11,)), pltpu.SemaphoreType.DMA((4,)), pltpu.SemaphoreType.DMA((4,)),
        ],
        compiler_params=pltpu.CompilerParams(
            collective_id=0, has_side_effects=True, vmem_limit_bytes=60 << 20
        ),
    )(
        inputs.reshape(1024, 128),
        diffusion,
        spectral.reshape(16, 32, 1024),
        pointwise,
        offsets,
        *tables(),
    )
    return out.reshape(32, 4, 8, 128)


def solution(mesh):
    return jax.shard_map(
        on_device,
        mesh=mesh,
        in_specs=(P(None, "gx", "gy", None), P("gx", "gy", None), P("gx", "gy", None, None, None), P(), P()),
        out_specs=P(None, "gx", "gy", None),
        check_vma=False,
    )
```

```python
import functools

import jax
import jax.numpy as jnp
import numpy as np
from jax import lax
from jax.experimental import pallas as pl
from jax.experimental.pallas import tpu as pltpu
from jax.sharding import PartitionSpec as P

MESH = pl.DeviceIdType.MESH
BF = jnp.bfloat16
F32 = jnp.float32

NT = (((1,), (1,)), ((), ()))
TN = (((0,), (0,)), ((), ()))
NN = (((1,), (0,)), ((), ()))


def mm(a, b, dims=NN):
    return lax.dot_general(a, b, dims, preferred_element_type=F32)


def freq(n):
    j = np.arange(n)
    return np.where(j < n // 2, j, j - n)


def turn(a, b, n):
    return 2.0 * np.pi / n * ((a * b) % n)


def parts(z):
    return np.stack([z.real, z.imag])


def tables():
    eye4, eye8 = np.eye(4), np.eye(8)
    z, kz = np.arange(128), np.arange(32)
    a = parts(np.exp(-1j * turn(kz[:, None], z[None, :], 128)))
    tz = np.einsum("rkz,xw->rkxwz", a, eye4).reshape(256, 512)
    x = 4 * (4 * np.arange(8)[None, :, None] + np.arange(4)[:, None, None]) + np.arange(4)
    kx = freq(64).reshape(32, 2).T
    th = turn(kx[None, None, None, :, :], x[:, :, :, None, None], 128)
    cs = np.stack([np.cos(th), np.sin(th)])
    tx = np.einsum("sZYxlg,cd->ZslgcYdx", cs, eye4).reshape(4, 512, 128)
    y = np.arange(32).reshape(4, 8)
    ky = freq(16).reshape(4, 4)
    ph = turn(y[:, :, None, None], ky[None, None], 32)
    unit = np.array([1.0, 1j])
    co = np.einsum("hyHk,s,r->hyHksr", np.exp(-1j * ph), np.conj(unit), unit)
    ty = np.einsum("qhyHksr,cd->shrcyHkqd", parts(co), eye8).reshape(1024, 256)
    txi = np.einsum("sZYxlg,cd->ZsYcxlgd", cs, eye4).reshape(4, 256, 256)
    co = np.einsum("HyhK,s,r->HyhKsr", np.exp(1j * ph), unit, unit)
    tyi = np.einsum("qHyhKsr,bd->shbKrHqdy", parts(co), eye8).reshape(512, 512)
    b = np.exp(1j * turn(kz[:, None], z[None, :], 128)) * 2.0**-7.5
    tzi = np.einsum("rkz,xw->rkxwz", np.stack([b.real, -b.imag]), eye4).reshape(256, 512)
    return [jnp.asarray(np.asarray(t, np.float32)).astype(BF) for t in (tz, tx, ty, txi, tyi, tzi)]


def iota(shape, dim):
    return lax.broadcasted_iota(jnp.int32, shape, dim)


def one_hot(cond):
    return jnp.where(cond, 1.0, 0.0).astype(BF)


def cells_by_x(x):
    wide = x.astype(F32).reshape(32, 4, 8, 128)
    return jnp.concatenate([wide[:, k].reshape(256, 128) for k in range(4)], axis=1)


def forward_z(xx, tz):
    out = mm(tz, xx, NT)
    res = []
    for q in range(4):
        lanes = slice(q * 64, q * 64 + 64)
        both = jnp.concatenate([out[:128, lanes], out[128:, lanes]], axis=1)
        res.append(both.astype(BF).reshape(32, 4, 128))
    return res


def before_gelu(wide, xx, diff, point, offset):
    rep = one_hot(iota((256, 32), 0) // 8 == iota((256, 32), 1))
    spread = mm(mm(rep, point).astype(BF), rep, NT)
    same_y = iota((256, 256), 0) % 8 == iota((256, 256), 1) % 8
    kron = jnp.where(same_y, spread, 0.0).astype(BF)
    mix = mm(kron, xx)
    gap = iota((128, 128), 0) - iota((128, 128), 1)
    sten = jnp.where(gap == 0, -2.0, jnp.where((gap == 1) | (gap == -1), 1.0, 0.0)).astype(BF)
    cols = []
    for k in range(4):
        lanes = slice(k * 128, k * 128 + 128)
        curv = mm(xx[:, lanes], sten).reshape(32, 8, 128)
        cols.append((curv * diff[k][None]).reshape(256, 128))
    shift = jnp.concatenate([jnp.full((8, 512), offset(o), F32) for o in range(32)], axis=0)
    return mix + jnp.concatenate(cols, axis=1) + shift


def forward_xy(r1, tx, ty):
    r1 = r1.reshape(512, 128)
    d = jnp.concatenate([r1[h * 128 : h * 128 + 128] for h in range(4)], axis=1)
    g = mm(tx, d).astype(BF)
    g = jnp.concatenate([g[:256], g[256:]], axis=1)
    o = mm(g, ty)
    res = []
    for h in range(4):
        lanes = slice(h * 64, h * 64 + 64)
        both = jnp.concatenate([o[:128, lanes], o[128:, lanes]], axis=1)
        res.append(both.astype(BF).reshape(32, 4, 128))
    return res


def own_modes(r2):
    r2 = r2.reshape(512, 128).astype(F32)
    u = r2[:128] + r2[128:256] + r2[256:384] + r2[384:]
    hi = u.astype(BF)
    lo = (u - hi.astype(F32)).astype(BF)
    row, col = iota((256, 512), 0), iota((256, 512), 1)
    row = row % 128
    rep = one_hot((row % 4 == col // 128) & (row // 4 == col % 32))
    return mm(jnp.concatenate([hi, lo], axis=0), rep, TN) * (2.0**-9.5)


def mix_modes(u, w):
    rows = []
    for j in range(8):
        wr, wi = w(2 * j).astype(F32), w(2 * j + 1).astype(F32)
        re = im = None
        for q in range(4):
            ur = jnp.concatenate([u[16 * j : 16 * j + 8, q * 128 : q * 128 + 128]] * 8, axis=1)
            ui = jnp.concatenate([u[16 * j + 8 : 16 * j + 16, q * 128 : q * 128 + 128]] * 8, axis=1)
            r, i = wr[q * 8 : q * 8 + 8], wi[q * 8 : q * 8 + 8]
            a, b = r * ur - i * ui, r * ui + i * ur
            re, im = (a, b) if re is None else (re + a, im + b)
        rows += [jnp.sum(re, axis=0, keepdims=True), jnp.sum(im, axis=0, keepdims=True)]
    y = jnp.concatenate(rows, axis=0)
    a = jnp.concatenate(
        [y[l * 8 : l * 8 + 8, b * 128 : b * 128 + 128] for l in range(2) for b in range(8)], axis=0
    ).astype(BF)
    row, col = iota((128, 128), 0), iota((128, 128), 1)
    perm = one_hot((row % 4 == col // 32) & (row // 4 == col % 32))
    return mm(perm, a, NT).astype(BF).reshape(32, 4, 128)


def inverse_xy(r3, txi, tyi):
    r3 = r3.reshape(512, 128)
    d = jnp.concatenate(
        [
            jnp.concatenate([r3[h * 128 : h * 128 + 128, l * 64 : l * 64 + 64] for h in range(4)], axis=1)
            for l in range(2)
        ],
        axis=0,
    )
    g = mm(txi, d).astype(BF)
    o = mm(jnp.concatenate([g[:128], g[128:]], axis=1), tyi).astype(BF)
    return [o[:, h * 128 : h * 128 + 128].reshape(8, 4, 4, 128) for h in range(4)]


def inverse_z(r4, tzi):
    halves = [
        jnp.concatenate([r4[o].reshape(128, 128)[:, r * 64 : r * 64 + 64] for o in range(4)], axis=1)
        for r in range(2)
    ]
    res = mm(jnp.concatenate(halves, axis=0), tzi, TN)
    return jnp.transpose(res.reshape(4, 8, 8, 512), (1, 0, 2, 3)).reshape(256, 512)


def gelu(v):
    return 0.5 * v * (1.0 + lax.erf(v * (0.5**0.5)))


def far_first(sizes):
    steps = [()]
    for n in sizes:
        steps = [s + (k,) for s in steps for k in range(n)]
    steps = [s + (c,) for s in steps for c in range(2)]
    steps.sort(key=lambda s: (-sum(min(k, n - k) for k, n in zip(s, sizes)), -s[-1]))
    return steps[:-1]


def kernel(
    x_hbm, diff_hbm, w_hbm, point_hbm, off_hbm, tz_hbm, tx_hbm, ty_hbm, txi_hbm, tyi_hbm, tzi_hbm,
    out_ref,
    x_v, diff_v, w_v, point_ref, off_ref, tz_v, tx_v, ty_v, txi_v, tyi_v, tzi_v, pre_v,
    s1, r1, s2, r2, s3, r3, s4, r4, load_sem, send_sem, recv_sem,
):
    g, h = lax.axis_index("gx"), lax.axis_index("gy")
    plane, zz = g // 4, g % 4
    kz = plane * 4 + h
    yy, xc, core = g // 8, (plane % 2) * 2 + h // 2, h % 2
    ys = [lax.rem(yy + k, 4) * 8 for k in range(4)]
    zs = [lax.rem(zz + k, 4) for k in range(4)]
    xs = [lax.rem(xc + k, 4) for k in range(4)]
    ups = [[ys[a] + xs[b] // 2 * 4 for b in range(4)] for a in range(4)]
    gys = [[xs[b] % 2 * 2 + c for c in (core, 1 - core)] for b in range(4)]
    everyone = [(ups[a][b] + zs[c], gys[b][d]) for a, b, c, d in far_first((4, 4, 4))]
    planar = [(ups[a][b], gys[b][d]) for a, b, d in far_first((4, 4))]

    barrier = pltpu.get_barrier_semaphore()
    for peer in everyone:
        pl.semaphore_signal(barrier, inc=1, device_id=peer, device_id_type=MESH)

    loads = [
        (x_hbm, x_v), (tz_hbm, tz_v), (diff_hbm, diff_v), (point_hbm, point_ref), (off_hbm, off_ref), (tx_hbm.at[zz], tx_v), (ty_hbm, ty_v),
        (w_hbm, w_v), (txi_hbm.at[zz], txi_v), (tyi_hbm, tyi_v), (tzi_hbm, tzi_v),
    ]
    loads = [pltpu.make_async_copy(a, b, load_sem.at[k]) for k, (a, b) in enumerate(loads)]
    for c in loads:
        c.start()
    loads[0].wait()
    loads[1].wait()
    xx = cells_by_x(x_v[...]).astype(BF)
    for q, block in enumerate(forward_z(xx, tz_v[...])):
        s1[:, q] = block
    for c in loads[2:5]:
        c.wait()
    diff = diff_v[...].astype(F32)
    pre_v[...] = before_gelu(None, xx, diff, point_ref[...], lambda o: off_ref[o])
    for c in loads[5:]:
        c.wait()
    pl.semaphore_wait(barrier, 127)

    def send(src, dst, phase, peer):
        pltpu.make_async_remote_copy(
            src, dst, send_sem.at[phase], recv_sem.at[phase], device_id=peer, device_id_type=MESH
        ).start()

    def wait(ref, sem):
        pltpu.make_async_copy(ref, ref, sem).wait()

    slot = h * 8 + plane
    for up, gy in planar:
        send(s1.at[up + gy], r1.at[slot], 0, (up + zz, gy))
    r1[slot] = s1[kz]
    wait(r1.at[pl.ds(0, 31)], recv_sem.at[0])

    for k, block in enumerate(forward_xy(r1[...], tx_v[...], ty_v[...])):
        s2[k] = block
    slot = zz * 32 + kz
    for gx, gy in everyone:
        send(s2.at[gy, gx], r2.at[slot], 1, (gx, gy))
    r2[slot] = s2[h, g]
    wait(r2.at[pl.ds(0, 127)], recv_sem.at[1])

    s3[...] = mix_modes(own_modes(r2[...]), lambda m: w_v[m])
    slot = h * 32 + g
    for a, b, c, d in far_first((4, 4, 4)):
        up, gy = ups[a][b], gys[b][d]
        send(s3.at[up + gy], r3.at[slot], 2, (up + zs[c], gy))
    r3[slot] = s3[kz]
    wait(r3.at[pl.ds(0, 127)], recv_sem.at[2])

    for k, block in enumerate(inverse_xy(r3[...], txi_v[...], tyi_v[...])):
        s4[:, k] = block
    for up, gy in planar:
        send(s4.at[up // 4, gy], r4.at[:, kz], 3, (up + zz, gy))
    r4[:, kz] = s4[plane, h]
    wait(r1.at[pl.ds(0, 31)], recv_sem.at[3])

    act = gelu(pre_v[...] + inverse_z(r4[...], tzi_v[...]))
    act = jnp.stack([act[:, k * 128 : k * 128 + 128].reshape(32, 8, 128) for k in range(4)], axis=1)
    out_ref[...] = act.reshape(1024, 128).astype(BF)

    wait(s1.at[pl.ds(0, 31)], send_sem.at[0])
    wait(r2.at[pl.ds(0, 127)], send_sem.at[1])
    wait(r2.at[pl.ds(0, 127)], send_sem.at[2])
    wait(s1.at[pl.ds(0, 31)], send_sem.at[3])


def on_device(inputs, diffusion, spectral, pointwise, offsets):
    hbm = pl.BlockSpec(memory_space=pltpu.HBM)
    vmem = pl.BlockSpec(memory_space=pltpu.VMEM)
    v = pltpu.VMEM
    args = [inputs.reshape(1024, 128), diffusion, spectral.reshape(16, 32, 1024), pointwise, offsets, *tables()]
    out = pl.pallas_call(
        kernel,
        out_shape=jax.ShapeDtypeStruct((1024, 128), BF),
        in_specs=[hbm] * 11,
        out_specs=vmem,
        scratch_shapes=[
            v((1024, 128), BF), v((4, 8, 128), BF), v((16, 32, 1024), BF), v((32, 32), BF), pltpu.SMEM((32,), F32),
            v((256, 512), BF), v((512, 128), BF), v((1024, 256), BF),
            v((256, 256), BF), v((512, 512), BF), v((256, 512), BF), v((256, 512), F32),
            v((32, 4, 4, 128), BF), v((32, 4, 4, 128), BF),
            v((4, 32, 4, 128), BF), v((128, 4, 128), BF),
            v((32, 4, 128), BF), v((128, 4, 128), BF),
            v((8, 4, 4, 4, 128), BF), v((4, 32, 4, 128), BF),
            pltpu.SemaphoreType.DMA((11,)), pltpu.SemaphoreType.DMA((4,)), pltpu.SemaphoreType.DMA((4,)),
        ],
        compiler_params=pltpu.CompilerParams(
            collective_id=0, has_side_effects=True, vmem_limit_bytes=40 << 20
        ),
    )(*[pltpu.with_memory_space_constraint(a, pltpu.HBM) for a in args])
    return out.reshape(32, 4, 8, 128)


def solution(mesh):
    return jax.shard_map(
        on_device,
        mesh=mesh,
        in_specs=(P(None, "gx", "gy", None), P("gx", "gy", None), P("gx", "gy", None, None, None), P(), P()),
        out_specs=P(None, "gx", "gy", None),
        check_vma=False,
    )
```

```python
import functools

import jax
import jax.numpy as jnp
import numpy as np
from jax import lax
from jax.experimental import pallas as pl
from jax.experimental.pallas import tpu as pltpu
from jax.sharding import PartitionSpec as P

MESH = pl.DeviceIdType.MESH
BF = jnp.bfloat16
F32 = jnp.float32

NT = (((1,), (1,)), ((), ()))
TN = (((0,), (0,)), ((), ()))
NN = (((1,), (0,)), ((), ()))


def mm(a, b, dims=NN):
    return lax.dot_general(a, b, dims, preferred_element_type=F32)


def freq(n):
    j = np.arange(n)
    return np.where(j < n // 2, j, j - n)


def turn(a, b, n):
    return 2.0 * np.pi / n * ((a * b) % n)


def parts(z):
    return np.stack([z.real, z.imag])


def tables():
    eye4, eye8 = np.eye(4), np.eye(8)
    z, kz = np.arange(128), np.arange(32)
    a = parts(np.exp(-1j * turn(kz[:, None], z[None, :], 128)))
    tz = np.einsum("rkz,xw->rkxwz", a, eye4).reshape(256, 512)
    unit = np.array([1.0, 1j])
    y = np.arange(32).reshape(4, 8)
    ky = freq(16).reshape(4, 4)
    ph = turn(y[:, :, None, None], ky[None, None], 32)
    co = np.einsum("hyHk,s,r->hyHksr", np.exp(-1j * ph), np.conj(unit), unit)
    ty = np.einsum("qhyHksr,cd->hrcysHkqd", parts(co), eye8).reshape(512, 512)
    x = 4 * (4 * np.arange(8)[None, :, None] + np.arange(4)[:, None, None]) + np.arange(4)
    kx = freq(64).reshape(32, 2).T
    th = turn(kx[None, None, None, :, :], x[:, :, :, None, None], 128)
    cs = np.stack([np.cos(th), np.sin(th)])
    tx = np.einsum("sZYxlg,cd->ZlgcsYdx", cs, eye4).reshape(4, 256, 256)
    txi = np.einsum("sZYxlg,cd->ZsYcxlgd", cs, eye4).reshape(4, 256, 256)
    co = np.einsum("HyhK,s,r->HyhKsr", np.exp(1j * ph), unit, unit)
    tyi = np.einsum("qHyhKsr,bd->shbKrHqdy", parts(co), eye8).reshape(512, 512)
    b = np.exp(1j * turn(kz[:, None], z[None, :], 128)) * 2.0**-7.5
    tzi = np.einsum("rkz,xw->rkxwz", np.stack([b.real, -b.imag]), eye4).reshape(256, 512)
    return [jnp.asarray(np.asarray(t, np.float32)).astype(BF) for t in (tz, tx, ty, txi, tyi, tzi)]


def iota(shape, dim):
    return lax.broadcasted_iota(jnp.int32, shape, dim)


def one_hot(cond):
    return jnp.where(cond, 1.0, 0.0).astype(BF)


def cells_by_x(x):
    wide = x.astype(F32).reshape(32, 4, 8, 128)
    return jnp.concatenate([wide[:, k].reshape(256, 128) for k in range(4)], axis=1)


def forward_z(xx, tz):
    out = mm(tz, xx, NT)
    res = []
    for q in range(4):
        lanes = slice(q * 64, q * 64 + 64)
        both = jnp.concatenate([out[:128, lanes], out[128:, lanes]], axis=1)
        res.append(both.astype(BF).reshape(32, 4, 128))
    return res


def before_gelu(wide, xx, diff, point, offset):
    rep = one_hot(iota((256, 32), 0) // 8 == iota((256, 32), 1))
    spread = mm(mm(rep, point).astype(BF), rep, NT)
    same_y = iota((256, 256), 0) % 8 == iota((256, 256), 1) % 8
    kron = jnp.where(same_y, spread, 0.0).astype(BF)
    mix = mm(kron, xx)
    gap = iota((128, 128), 0) - iota((128, 128), 1)
    sten = jnp.where(gap == 0, -2.0, jnp.where((gap == 1) | (gap == -1), 1.0, 0.0)).astype(BF)
    cols = []
    for k in range(4):
        lanes = slice(k * 128, k * 128 + 128)
        curv = mm(xx[:, lanes], sten).reshape(32, 8, 128)
        cols.append((curv * diff[k][None]).reshape(256, 128))
    shift = jnp.concatenate([jnp.full((8, 512), offset(o), F32) for o in range(32)], axis=0)
    return mix + jnp.concatenate(cols, axis=1) + shift


def forward_xy(r1, tx, ty):
    r1 = r1.reshape(512, 128)
    d = jnp.concatenate([r1[h * 128 : h * 128 + 128] for h in range(4)], axis=1)
    e = mm(d, ty).astype(BF)
    o = mm(tx, jnp.concatenate([e[:, :256], e[:, 256:]], axis=0))
    res = []
    for h in range(4):
        lanes = slice(h * 64, h * 64 + 64)
        both = jnp.concatenate([o[:128, lanes], o[128:, lanes]], axis=1)
        res.append(both.astype(BF).reshape(32, 4, 128))
    return res


def own_modes(r2):
    r2 = r2.reshape(512, 128).astype(F32)
    u = r2[:128] + r2[128:256] + r2[256:384] + r2[384:]
    hi = u.astype(BF)
    lo = (u - hi.astype(F32)).astype(BF)
    row, col = iota((256, 512), 0), iota((256, 512), 1)
    row = row % 128
    rep = one_hot((row % 4 == col // 128) & (row // 4 == col % 32))
    return mm(jnp.concatenate([hi, lo], axis=0), rep, TN) * (2.0**-9.5)


def sum_rows(acc):
    row = iota(acc[0].shape, 0)
    half = row < 4
    four = [
        jnp.where(half, acc[k], acc[k + 4]) + pltpu.roll(jnp.where(half, acc[k + 4], acc[k]), 4, 0)
        for k in range(4)
    ]

    def join(a, b, k):
        return jnp.where(row % (2 * k) < k, a + pltpu.roll(a, 8 - k, 0), b + pltpu.roll(b, k, 0))

    return join(join(four[0], four[2], 2), join(four[1], four[3], 2), 1)


def mix_modes(u, w):
    blocks = []
    for l in range(2):
        acc = []
        for j in range(4 * l, 4 * l + 4):
            wr, wi = w(2 * j), w(2 * j + 1)
            re = im = None
            for q in range(4):
                ur = jnp.concatenate([u[16 * j : 16 * j + 8, q * 128 : q * 128 + 128]] * 8, axis=1)
                ui = jnp.concatenate([u[16 * j + 8 : 16 * j + 16, q * 128 : q * 128 + 128]] * 8, axis=1)
                r, i = wr[q * 8 : q * 8 + 8], wi[q * 8 : q * 8 + 8]
                a, b = r * ur - i * ui, r * ui + i * ur
                re, im = (a, b) if re is None else (re + a, im + b)
            acc += [re, im]
        y = sum_rows(acc)
        blocks += [y[:, b * 128 : b * 128 + 128] for b in range(8)]
    a = jnp.concatenate(blocks, axis=0).astype(BF)
    row, col = iota((128, 128), 0), iota((128, 128), 1)
    perm = one_hot((row % 4 == col // 32) & (row // 4 == col % 32))
    return mm(perm, a, NT).astype(BF).reshape(32, 4, 128)


def inverse_xy(r3, txi, tyi):
    r3 = r3.reshape(512, 128)
    d = jnp.concatenate(
        [
            jnp.concatenate([r3[h * 128 : h * 128 + 128, l * 64 : l * 64 + 64] for h in range(4)], axis=1)
            for l in range(2)
        ],
        axis=0,
    )
    g = mm(txi, d).astype(BF)
    o = mm(jnp.concatenate([g[:128], g[128:]], axis=1), tyi).astype(BF)
    return [o[:, h * 128 : h * 128 + 128].reshape(8, 4, 4, 128) for h in range(4)]


def inverse_z(r4, tzi):
    halves = [
        jnp.concatenate([r4[o].reshape(128, 128)[:, r * 64 : r * 64 + 64] for o in range(4)], axis=1)
        for r in range(2)
    ]
    res = mm(jnp.concatenate(halves, axis=0), tzi, TN)
    return jnp.transpose(res.reshape(4, 8, 8, 512), (1, 0, 2, 3)).reshape(256, 512)


def gelu(v):
    return 0.5 * v * (1.0 + lax.erf(v * (0.5**0.5)))


def far_first(sizes):
    steps = [()]
    for n in sizes:
        steps = [s + (k,) for s in steps for k in range(n)]
    steps = [s + (c,) for s in steps for c in range(2)]
    steps.sort(key=lambda s: (-sum(min(k, n - k) for k, n in zip(s, sizes)), -s[-1]))
    return steps[:-1]


def kernel(
    x_hbm, diff_hbm, w_hbm, point_hbm, off_hbm, tz_hbm, tx_hbm, ty_hbm, txi_hbm, tyi_hbm, tzi_hbm,
    out_ref,
    x_v, diff_v, w_v, wide_v, point_ref, off_ref, tz_v, tx_v, ty_v, txi_v, tyi_v, tzi_v, pre_v,
    s1, r1, s2, r2, s3, r3, s4, r4, load_sem, send_sem, recv_sem,
):
    g, h = lax.axis_index("gx"), lax.axis_index("gy")
    plane, zz = g // 4, g % 4
    kz = plane * 4 + h
    yy, xc, core = g // 8, (plane % 2) * 2 + h // 2, h % 2
    ys = [lax.rem(yy + k, 4) * 8 for k in range(4)]
    zs = [lax.rem(zz + k, 4) for k in range(4)]
    xs = [lax.rem(xc + k, 4) for k in range(4)]
    ups = [[ys[a] + xs[b] // 2 * 4 for b in range(4)] for a in range(4)]
    gys = [[xs[b] % 2 * 2 + c for c in (core, 1 - core)] for b in range(4)]
    everyone = [(ups[a][b] + zs[c], gys[b][d]) for a, b, c, d in far_first((4, 4, 4))]
    planar = [(ups[a][b], gys[b][d]) for a, b, d in far_first((4, 4))]

    barrier = pltpu.get_barrier_semaphore()
    for peer in everyone:
        pl.semaphore_signal(barrier, inc=1, device_id=peer, device_id_type=MESH)

    loads = [
        (x_hbm, x_v), (tz_hbm, tz_v), (diff_hbm, diff_v), (point_hbm, point_ref), (off_hbm, off_ref), (tx_hbm.at[zz], tx_v), (ty_hbm, ty_v),
        (w_hbm, w_v), (txi_hbm.at[zz], txi_v), (tyi_hbm, tyi_v), (tzi_hbm, tzi_v),
    ]
    loads = [pltpu.make_async_copy(a, b, load_sem.at[k]) for k, (a, b) in enumerate(loads)]
    for c in loads:
        c.start()
    loads[0].wait()
    loads[1].wait()
    xx = cells_by_x(x_v[...]).astype(BF)
    for q, block in enumerate(forward_z(xx, tz_v[...])):
        s1[:, q] = block
    for c in loads[2:5]:
        c.wait()
    diff = diff_v[...].astype(F32)
    pre_v[...] = before_gelu(None, xx, diff, point_ref[...], lambda o: off_ref[o])
    for c in loads[5:]:
        c.wait()
    pl.semaphore_wait(barrier, 127)

    def send(src, dst, phase, peer):
        pltpu.make_async_remote_copy(
            src, dst, send_sem.at[phase], recv_sem.at[phase], device_id=peer, device_id_type=MESH
        ).start()

    def wait(ref, sem):
        pltpu.make_async_copy(ref, ref, sem).wait()

    slot = h * 8 + plane
    for up, gy in planar:
        send(s1.at[up + gy], r1.at[slot], 0, (up + zz, gy))
    r1[slot] = s1[kz]
    for m in range(16):
        wide_v[m] = w_v[m].astype(F32)
    wait(r1.at[pl.ds(0, 31)], recv_sem.at[0])

    for k, block in enumerate(forward_xy(r1[...], tx_v[...], ty_v[...])):
        s2[k] = block
    slot = zz * 32 + kz
    for gx, gy in everyone:
        send(s2.at[gy, gx], r2.at[slot], 1, (gx, gy))
    r2[slot] = s2[h, g]
    wait(r2.at[pl.ds(0, 127)], recv_sem.at[1])

    s3[...] = mix_modes(own_modes(r2[...]), lambda m: wide_v[m])
    slot = h * 32 + g
    for a, b, c, d in far_first((4, 4, 4)):
        up, gy = ups[a][b], gys[b][d]
        send(s3.at[up + gy], r3.at[slot], 2, (up + zs[c], gy))
    r3[slot] = s3[kz]
    wait(r3.at[pl.ds(0, 127)], recv_sem.at[2])

    for k, block in enumerate(inverse_xy(r3[...], txi_v[...], tyi_v[...])):
        s4[:, k] = block
    for up, gy in planar:
        send(s4.at[up // 4, gy], r4.at[:, kz], 3, (up + zz, gy))
    r4[:, kz] = s4[plane, h]
    wait(r1.at[pl.ds(0, 31)], recv_sem.at[3])

    act = gelu(pre_v[...] + inverse_z(r4[...], tzi_v[...]))
    act = jnp.stack([act[:, k * 128 : k * 128 + 128].reshape(32, 8, 128) for k in range(4)], axis=1)
    out_ref[...] = act.reshape(1024, 128).astype(BF)

    wait(s1.at[pl.ds(0, 31)], send_sem.at[0])
    wait(r2.at[pl.ds(0, 127)], send_sem.at[1])
    wait(r2.at[pl.ds(0, 127)], send_sem.at[2])
    wait(s1.at[pl.ds(0, 31)], send_sem.at[3])


def on_device(inputs, diffusion, spectral, pointwise, offsets):
    hbm = pl.BlockSpec(memory_space=pltpu.HBM)
    vmem = pl.BlockSpec(memory_space=pltpu.VMEM)
    v = pltpu.VMEM
    args = [inputs.reshape(1024, 128), diffusion, spectral.reshape(16, 32, 1024), pointwise, offsets, *tables()]
    out = pl.pallas_call(
        kernel,
        out_shape=jax.ShapeDtypeStruct((1024, 128), BF),
        in_specs=[hbm] * 11,
        out_specs=vmem,
        scratch_shapes=[
            v((1024, 128), BF), v((4, 8, 128), BF), v((16, 32, 1024), BF), v((16, 32, 1024), F32), v((32, 32), BF), pltpu.SMEM((32,), F32),
            v((256, 512), BF), v((256, 256), BF), v((512, 512), BF),
            v((256, 256), BF), v((512, 512), BF), v((256, 512), BF), v((256, 512), F32),
            v((32, 4, 4, 128), BF), v((32, 4, 4, 128), BF),
            v((4, 32, 4, 128), BF), v((128, 4, 128), BF),
            v((32, 4, 128), BF), v((128, 4, 128), BF),
            v((8, 4, 4, 4, 128), BF), v((4, 32, 4, 128), BF),
            pltpu.SemaphoreType.DMA((11,)), pltpu.SemaphoreType.DMA((4,)), pltpu.SemaphoreType.DMA((4,)),
        ],
        compiler_params=pltpu.CompilerParams(
            collective_id=0, has_side_effects=True, vmem_limit_bytes=40 << 20
        ),
    )(*[pltpu.with_memory_space_constraint(a, pltpu.HBM) for a in args])
    return out.reshape(32, 4, 8, 128)


def solution(mesh):
    return jax.shard_map(
        on_device,
        mesh=mesh,
        in_specs=(P(None, "gx", "gy", None), P("gx", "gy", None), P("gx", "gy", None, None, None), P(), P()),
        out_specs=P(None, "gx", "gy", None),
        check_vma=False,
    )
```

```python
import functools

import jax
import jax.numpy as jnp
import numpy as np
from jax import lax
from jax.experimental import pallas as pl
from jax.experimental.pallas import tpu as pltpu
from jax.sharding import PartitionSpec as P

MESH = pl.DeviceIdType.MESH
BF = jnp.bfloat16
F32 = jnp.float32

NT = (((1,), (1,)), ((), ()))
TN = (((0,), (0,)), ((), ()))
NN = (((1,), (0,)), ((), ()))


def mm(a, b, dims=NN):
    return lax.dot_general(a, b, dims, preferred_element_type=F32)


def freq(n):
    j = np.arange(n)
    return np.where(j < n // 2, j, j - n)


def turn(a, b, n):
    return 2.0 * np.pi / n * ((a * b) % n)


def parts(z):
    return np.stack([z.real, z.imag])


def tables():
    eye4, eye8 = np.eye(4), np.eye(8)
    z, kz = np.arange(128), np.arange(32)
    a = parts(np.exp(-1j * turn(kz[:, None], z[None, :], 128)))
    tz = np.einsum("rkz,xw->rkxwz", a, eye4).reshape(256, 512)
    unit = np.array([1.0, 1j])
    y = np.arange(32).reshape(4, 8)
    ky = freq(16).reshape(4, 4)
    ph = turn(y[:, :, None, None], ky[None, None], 32)
    co = np.einsum("hyHk,s,r->hyHksr", np.exp(-1j * ph), np.conj(unit), unit)
    ty = np.einsum("qhyHksr,cd->hrcysHkqd", parts(co), eye8).reshape(512, 512)
    x = 4 * (4 * np.arange(8)[None, :, None] + np.arange(4)[:, None, None]) + np.arange(4)
    kx = np.transpose(freq(64).reshape(4, 8, 2), (0, 2, 1))
    th = turn(kx[None, None, None], x[:, :, :, None, None, None], 128)
    cs = np.stack([np.cos(th), np.sin(th)])
    tx = np.einsum("sZYxylg,cd->ZylgcsYdx", cs, eye4).reshape(4, 4, 64, 256)
    cs = cs.reshape(2, 4, 4, 2, 4, 4, 2, 8)
    txi = np.einsum("sZYhxylg,cd->ZYshcxlygd", cs, eye4).reshape(4, 4, 64, 256)
    co = np.einsum("HyhK,s,r->HyhKsr", np.exp(1j * ph), unit, unit)
    tyi = np.einsum("qHyhKsr,bd->shbKrHqdy", parts(co), eye8).reshape(512, 512)
    b = np.exp(1j * turn(kz[:, None], z[None, :], 128)) * 2.0**-7.5
    tzi = np.einsum("rkz,xw->rkxwz", np.stack([b.real, -b.imag]), eye4).reshape(256, 512)
    return [jnp.asarray(np.asarray(t, np.float32)).astype(BF) for t in (tz, tx, ty, txi, tyi, tzi)]


def iota(shape, dim):
    return lax.broadcasted_iota(jnp.int32, shape, dim)


def one_hot(cond):
    return jnp.where(cond, 1.0, 0.0).astype(BF)


def cells_by_x(x):
    wide = x.astype(F32).reshape(32, 4, 8, 128)
    return jnp.concatenate([wide[:, k].reshape(256, 128) for k in range(4)], axis=1)


def forward_z(xx, tz):
    out = mm(tz, xx, NT)
    res = []
    for q in range(4):
        lanes = slice(q * 64, q * 64 + 64)
        both = jnp.concatenate([out[:128, lanes], out[128:, lanes]], axis=1)
        res.append(both.astype(BF).reshape(32, 4, 128))
    return res


def before_gelu(wide, xx, diff, point, offset):
    rep = one_hot(iota((256, 32), 0) // 8 == iota((256, 32), 1))
    spread = mm(mm(rep, point).astype(BF), rep, NT)
    same_y = iota((256, 256), 0) % 8 == iota((256, 256), 1) % 8
    kron = jnp.where(same_y, spread, 0.0).astype(BF)
    mix = mm(kron, xx)
    gap = iota((128, 128), 0) - iota((128, 128), 1)
    sten = jnp.where(gap == 0, -2.0, jnp.where((gap == 1) | (gap == -1), 1.0, 0.0)).astype(BF)
    cols = []
    for k in range(4):
        lanes = slice(k * 128, k * 128 + 128)
        curv = mm(xx[:, lanes], sten).reshape(32, 8, 128)
        cols.append((curv * diff[k][None]).reshape(256, 128))
    shift = jnp.concatenate([jnp.full((8, 512), offset(o), F32) for o in range(32)], axis=0)
    return mix + jnp.concatenate(cols, axis=1) + shift


def forward_y(r1, ty):
    r1 = r1.reshape(512, 128)
    d = jnp.concatenate([r1[h * 128 : h * 128 + 128] for h in range(4)], axis=1)
    e = mm(d, ty).astype(BF)
    return jnp.concatenate([e[:, :256], e[:, 256:]], axis=0)


def forward_x(e, tx):
    o = mm(jnp.concatenate(tx, axis=0), e)
    res = []
    for k in range(len(tx)):
        lo, hi = o[k * 64 : k * 64 + 32], o[k * 64 + 32 : k * 64 + 64]
        both = [jnp.concatenate([lo[:, h * 64 : h * 64 + 64], hi[:, h * 64 : h * 64 + 64]], axis=1) for h in range(4)]
        res.append([b.astype(BF).reshape(8, 4, 128) for b in both])
    return res


def spread_table():
    row, col = iota((256, 512), 0) % 128, iota((256, 512), 1)
    return one_hot((row % 4 == col // 128) & (row // 4 == col % 32))


def order_table():
    row, col = iota((128, 128), 0), iota((128, 128), 1)
    return one_hot((row % 4 == col // 32) & (row // 4 == col % 32))


def own_modes(r2, spread):
    r2 = r2.reshape(512, 128).astype(F32)
    u = r2[:128] + r2[128:256] + r2[256:384] + r2[384:]
    hi = u.astype(BF)
    lo = (u - hi.astype(F32)).astype(BF)
    return mm(jnp.concatenate([hi, lo], axis=0), spread, TN) * (2.0**-9.5)


def sum_rows(acc):
    row = iota(acc[0].shape, 0)
    half = row < 4
    four = [
        jnp.where(half, acc[k], acc[k + 4]) + pltpu.roll(jnp.where(half, acc[k + 4], acc[k]), 4, 0)
        for k in range(4)
    ]

    def join(a, b, k):
        return jnp.where(row % (2 * k) < k, a + pltpu.roll(a, 8 - k, 0), b + pltpu.roll(b, k, 0))

    return join(join(four[0], four[2], 2), join(four[1], four[3], 2), 1)


def mix_modes(u, w, order):
    blocks = []
    for l in range(2):
        acc = []
        for j in range(4 * l, 4 * l + 4):
            wr, wi = w(2 * j), w(2 * j + 1)
            re = im = None
            for q in range(4):
                ur = jnp.concatenate([u[16 * j : 16 * j + 8, q * 128 : q * 128 + 128]] * 8, axis=1)
                ui = jnp.concatenate([u[16 * j + 8 : 16 * j + 16, q * 128 : q * 128 + 128]] * 8, axis=1)
                r, i = wr[q * 8 : q * 8 + 8], wi[q * 8 : q * 8 + 8]
                a, b = r * ur - i * ui, r * ui + i * ur
                re, im = (a, b) if re is None else (re + a, im + b)
            acc += [re, im]
        y = sum_rows(acc)
        blocks += [y[:, b * 128 : b * 128 + 128] for b in range(8)]
    a = jnp.concatenate(blocks, axis=0).astype(BF)
    return mm(order, a, NT).astype(BF).reshape(32, 4, 128)


def modes_by_kx(r3):
    r3 = r3.reshape(512, 128)
    return jnp.concatenate(
        [
            jnp.concatenate([r3[h * 128 : h * 128 + 128, l * 64 : l * 64 + 64] for h in range(4)], axis=1)
            for l in range(2)
        ],
        axis=0,
    )


def inverse_xy(d, txi, tyi):
    g = mm(jnp.concatenate(txi, axis=0), d).astype(BF)
    g = [jnp.concatenate([g[k * 64 : k * 64 + 32], g[k * 64 + 32 : k * 64 + 64]], axis=1) for k in range(len(txi))]
    o = mm(jnp.concatenate(g, axis=0), tyi).astype(BF)
    return [
        [o[k * 32 : k * 32 + 32, h * 128 : h * 128 + 128].reshape(2, 4, 4, 128) for h in range(4)]
        for k in range(len(txi))
    ]


def inverse_z(r4, tzi):
    halves = [
        jnp.concatenate([r4[:, o].reshape(128, 128)[:, r * 64 : r * 64 + 64] for o in range(4)], axis=1)
        for r in range(2)
    ]
    res = mm(jnp.concatenate(halves, axis=0), tzi, TN)
    return jnp.transpose(res.reshape(4, 8, 8, 512), (1, 0, 2, 3)).reshape(256, 512)


def gelu(v):
    return 0.5 * v * (1.0 + lax.erf(v * (0.5**0.5)))


def far_first(sizes):
    steps = [()]
    for n in sizes:
        steps = [s + (k,) for s in steps for k in range(n)]
    steps = [s + (c,) for s in steps for c in range(2)]
    steps.sort(key=lambda s: (-sum(min(k, n - k) for k, n in zip(s, sizes)), -s[-1]))
    return steps[:-1]


def kernel(
    x_hbm, diff_hbm, w_hbm, point_hbm, off_hbm, tz_hbm, tx_hbm, ty_hbm, txi_hbm, tyi_hbm, tzi_hbm,
    out_ref,
    x_v, diff_v, w_v, wide_v, spread_v, order_v, point_ref, off_ref, tz_v, tx_v, ty_v, txi_v, tyi_v, tzi_v, pre_v,
    s1, r1, s2, r2, s3, r3, s4, r4, load_sem, send_sem, recv_sem,
):
    g, h = lax.axis_index("gx"), lax.axis_index("gy")
    plane, zz = g // 4, g % 4
    kz = plane * 4 + h
    yy, xc, core = g // 8, (plane % 2) * 2 + h // 2, h % 2
    ys = [lax.rem(yy + k, 4) for k in range(4)]
    zs = [lax.rem(zz + k, 4) for k in range(4)]
    xs = [lax.rem(xc + k, 4) for k in range(4)]
    xhs = [xs[b] // 2 for b in range(4)]
    ups = [[ys[a] * 8 + xhs[b] * 4 for b in range(4)] for a in range(4)]
    gys = [[xs[b] % 2 * 2 + c for c in (core, 1 - core)] for b in range(4)]
    everyone = [(ups[a][b] + zs[c], gys[b][d]) for a, b, c, d in far_first((4, 4, 4))]
    planar = [(ups[a][b], gys[b][d]) for a, b, d in far_first((4, 4))]

    barrier = pltpu.get_barrier_semaphore()
    for peer in everyone:
        pl.semaphore_signal(barrier, inc=1, device_id=peer, device_id_type=MESH)

    loads = [
        (x_hbm, x_v), (tz_hbm, tz_v), (diff_hbm, diff_v), (point_hbm, point_ref), (off_hbm, off_ref), (tx_hbm.at[zz], tx_v), (ty_hbm, ty_v),
        (w_hbm, w_v), (txi_hbm.at[zz], txi_v), (tyi_hbm, tyi_v), (tzi_hbm, tzi_v),
    ]
    loads = [pltpu.make_async_copy(a, b, load_sem.at[k]) for k, (a, b) in enumerate(loads)]
    for c in loads:
        c.start()
    loads[0].wait()
    loads[1].wait()
    xx = cells_by_x(x_v[...]).astype(BF)
    for q, block in enumerate(forward_z(xx, tz_v[...])):
        s1[:, q] = block
    for c in loads[2:5]:
        c.wait()
    diff = diff_v[...].astype(F32)
    pre_v[...] = before_gelu(None, xx, diff, point_ref[...], lambda o: off_ref[o])
    for c in loads[5:]:
        c.wait()
    pl.semaphore_wait(barrier, 127)

    def send(src, dst, phase, peer):
        pltpu.make_async_remote_copy(
            src, dst, send_sem.at[phase], recv_sem.at[phase], device_id=peer, device_id_type=MESH
        ).start()

    def wait(ref, sem):
        pltpu.make_async_copy(ref, ref, sem).wait()

    slot = h * 8 + plane
    for up, gy in planar:
        send(s1.at[up + gy], r1.at[slot], 0, (up + zz, gy))
    r1[slot] = s1[kz]
    spread_v[...] = spread_table()
    order_v[...] = order_table()
    for m in range(16):
        wide_v[m] = w_v[m].astype(F32)
    wait(r1.at[pl.ds(0, 31)], recv_sem.at[0])

    e = forward_y(r1[...], ty_v[...])
    slot = zz * 32 + kz
    for near in ((2, 1), (3, 0)):
        for k, blocks in zip(near, forward_x(e, [tx_v[ys[k]] for k in near])):
            for j, block in enumerate(blocks):
                s2[j, ys[k]] = block
        for a, b, c, d in far_first((4, 4, 4)):
            if a in near:
                up, gy = xhs[b] * 4 + zs[c], gys[b][d]
                send(s2.at[gy, ys[a], up], r2.at[slot], 1, (ys[a] * 8 + up, gy))
    r2[slot] = s2[h, yy, g % 8]
    wait(r2.at[pl.ds(0, 127)], recv_sem.at[1])

    s3[...] = mix_modes(own_modes(r2[...], spread_v[...]), lambda m: wide_v[m], order_v[...])
    slot = h * 32 + g
    for a, b, c, d in far_first((4, 4, 4)):
        up, gy = ups[a][b], gys[b][d]
        send(s3.at[up + gy], r3.at[slot], 2, (up + zs[c], gy))
    r3[slot] = s3[kz]
    wait(r3.at[pl.ds(0, 127)], recv_sem.at[2])

    modes = modes_by_kx(r3[...])
    for near in ((2, 1), (3, 0)):
        for k, blocks in zip(near, inverse_xy(modes, [txi_v[ys[k]] for k in near], tyi_v[...])):
            for j, block in enumerate(blocks):
                s4[ys[k], :, j] = block
        for a, b, d in far_first((4, 4)):
            if a in near:
                send(s4.at[ys[a], xhs[b], gys[b][d]], r4.at[kz], 3, (ups[a][b] + zz, gys[b][d]))
    r4[kz] = s4[yy, plane % 2, h]
    wait(r1.at[pl.ds(0, 31)], recv_sem.at[3])

    act = gelu(pre_v[...] + inverse_z(r4[...], tzi_v[...]))
    act = jnp.stack([act[:, k * 128 : k * 128 + 128].reshape(32, 8, 128) for k in range(4)], axis=1)
    out_ref[...] = act.reshape(1024, 128).astype(BF)

    wait(s1.at[pl.ds(0, 31)], send_sem.at[0])
    wait(r2.at[pl.ds(0, 127)], send_sem.at[1])
    wait(r2.at[pl.ds(0, 127)], send_sem.at[2])
    wait(s1.at[pl.ds(0, 31)], send_sem.at[3])


def on_device(inputs, diffusion, spectral, pointwise, offsets):
    hbm = pl.BlockSpec(memory_space=pltpu.HBM)
    vmem = pl.BlockSpec(memory_space=pltpu.VMEM)
    v = pltpu.VMEM
    args = [inputs.reshape(1024, 128), diffusion, spectral.reshape(16, 32, 1024), pointwise, offsets, *tables()]
    out = pl.pallas_call(
        kernel,
        out_shape=jax.ShapeDtypeStruct((1024, 128), BF),
        in_specs=[hbm] * 11,
        out_specs=vmem,
        scratch_shapes=[
            v((1024, 128), BF), v((4, 8, 128), BF), v((16, 32, 1024), BF), v((16, 32, 1024), F32), v((256, 512), BF), v((128, 128), BF), v((32, 32), BF), pltpu.SMEM((32,), F32),
            v((256, 512), BF), v((4, 64, 256), BF), v((512, 512), BF),
            v((4, 64, 256), BF), v((512, 512), BF), v((256, 512), BF), v((256, 512), F32),
            v((32, 4, 4, 128), BF), v((32, 4, 4, 128), BF),
            v((4, 4, 8, 4, 128), BF), v((128, 4, 128), BF),
            v((32, 4, 128), BF), v((128, 4, 128), BF),
            v((4, 2, 4, 4, 4, 128), BF), v((32, 4, 4, 128), BF),
            pltpu.SemaphoreType.DMA((11,)), pltpu.SemaphoreType.DMA((4,)), pltpu.SemaphoreType.DMA((4,)),
        ],
        compiler_params=pltpu.CompilerParams(
            collective_id=0, has_side_effects=True, vmem_limit_bytes=40 << 20
        ),
    )(*[pltpu.with_memory_space_constraint(a, pltpu.HBM) for a in args])
    return out.reshape(32, 4, 8, 128)


def solution(mesh):
    return jax.shard_map(
        on_device,
        mesh=mesh,
        in_specs=(P(None, "gx", "gy", None), P("gx", "gy", None), P("gx", "gy", None, None, None), P(), P()),
        out_specs=P(None, "gx", "gy", None),
        check_vma=False,
    )
```

```python
import functools

import jax
import jax.numpy as jnp
import ml_dtypes
import numpy as np
from jax import lax
from jax.experimental import pallas as pl
from jax.experimental.pallas import tpu as pltpu
from jax.sharding import PartitionSpec as P

MESH = pl.DeviceIdType.MESH
BF = jnp.bfloat16
F32 = jnp.float32

NT = (((1,), (1,)), ((), ()))
TN = (((0,), (0,)), ((), ()))
NN = (((1,), (0,)), ((), ()))


def mm(a, b, dims=NN):
    return lax.dot_general(a, b, dims, preferred_element_type=F32)


def freq(n):
    j = np.arange(n)
    return np.where(j < n // 2, j, j - n)


def turn(a, b, n):
    return 2.0 * np.pi / n * ((a * b) % n)


def parts(z):
    return np.stack([z.real, z.imag])


def two_parts(t, axis, order):
    high = np.asarray(t, np.float32).astype(ml_dtypes.bfloat16).astype(np.float64)
    return np.concatenate([(high, t - high)[k] for k in order], axis=axis)


def tables():
    eye4, eye8 = np.eye(4), np.eye(8)
    z, kz = np.arange(128), np.arange(32)
    a = parts(np.exp(-1j * turn(kz[:, None], z[None, :], 128)))
    tz = np.einsum("rkz,xw->rkxwz", a, eye4).reshape(256, 512)
    unit = np.array([1.0, 1j])
    y = np.arange(32).reshape(4, 8)
    ky = freq(16).reshape(4, 4)
    ph = turn(y[:, :, None, None], ky[None, None], 32)
    co = np.einsum("hyHk,s,r->hyHksr", np.exp(-1j * ph), np.conj(unit), unit)
    ty = np.einsum("qhyHksr,cd->hrcysHkqd", parts(co), eye8).reshape(512, 512)
    x = 4 * (4 * np.arange(8)[None, :, None] + np.arange(4)[:, None, None]) + np.arange(4)
    kx = np.transpose(freq(64).reshape(4, 8, 2), (0, 2, 1))
    th = turn(kx[None, None, None], x[:, :, :, None, None, None], 128)
    cs = np.stack([np.cos(th), np.sin(th)])
    tx = np.einsum("sZYxylg,cd->ZylgcsYdx", cs, eye4).reshape(4, 4, 64, 256)
    cs = cs.reshape(2, 4, 4, 2, 4, 4, 2, 8)
    txi = np.einsum("sZYhxylg,cd->ZYshcxlygd", cs, eye4).reshape(4, 4, 64, 256)
    co = np.einsum("HyhK,s,r->HyhKsr", np.exp(1j * ph), unit, unit)
    tyi = np.einsum("qHyhKsr,bd->shbKrHqdy", parts(co), eye8).reshape(512, 512)
    b = np.exp(1j * turn(kz[:, None], z[None, :], 128)) * 2.0**-7.5
    tzi = np.einsum("rkz,xw->rkxwz", np.stack([b.real, -b.imag]), eye4).reshape(256, 512)
    tx, txi = two_parts(tx, 3, (0, 1, 0)), two_parts(txi, 3, (0, 1))
    tzi = two_parts(tzi, 0, (0, 1))
    return [jnp.asarray(np.asarray(t, np.float32).astype(ml_dtypes.bfloat16)) for t in (tz, tx, ty, txi, tyi, tzi)]


def iota(shape, dim):
    return lax.broadcasted_iota(jnp.int32, shape, dim)


def one_hot(cond):
    return jnp.where(cond, 1.0, 0.0).astype(BF)


def cells_by_x(x):
    wide = x.astype(F32).reshape(32, 4, 8, 128)
    return jnp.concatenate([wide[:, k].reshape(256, 128) for k in range(4)], axis=1)


def forward_z(xx, tz):
    out = mm(tz, xx, NT)
    res = []
    for q in range(4):
        lanes = slice(q * 64, q * 64 + 64)
        both = jnp.concatenate([out[:128, lanes], out[128:, lanes]], axis=1)
        res.append(both.astype(BF).reshape(32, 4, 128))
    return res


def before_gelu(wide, xx, diff, point, offset):
    rep = one_hot(iota((256, 32), 0) // 8 == iota((256, 32), 1))
    spread = mm(mm(rep, point).astype(BF), rep, NT)
    same_y = iota((256, 256), 0) % 8 == iota((256, 256), 1) % 8
    kron = jnp.where(same_y, spread, 0.0).astype(BF)
    mix = mm(kron, xx)
    gap = iota((128, 128), 0) - iota((128, 128), 1)
    sten = jnp.where(gap == 0, -2.0, jnp.where((gap == 1) | (gap == -1), 1.0, 0.0)).astype(BF)
    cols = []
    for k in range(4):
        lanes = slice(k * 128, k * 128 + 128)
        curv = mm(xx[:, lanes], sten).reshape(32, 8, 128)
        cols.append((curv * diff[k][None]).reshape(256, 128))
    shift = jnp.concatenate([jnp.full((8, 512), offset(o), F32) for o in range(32)], axis=0)
    return mix + jnp.concatenate(cols, axis=1) + shift


def forward_y(r1, ty):
    r1 = r1.reshape(512, 128)
    d = jnp.concatenate([r1[h * 128 : h * 128 + 128] for h in range(4)], axis=1)
    e = mm(d, ty)
    e = jnp.concatenate([e[:, :256], e[:, 256:]], axis=0)
    high = e.astype(BF)
    return jnp.concatenate([high, high, (e - high.astype(F32)).astype(BF)], axis=0)


def forward_x(e, tx):
    o = mm(jnp.concatenate(tx, axis=0), e)
    res = []
    for k in range(len(tx)):
        lo, hi = o[k * 64 : k * 64 + 32], o[k * 64 + 32 : k * 64 + 64]
        both = [jnp.concatenate([lo[:, h * 64 : h * 64 + 64], hi[:, h * 64 : h * 64 + 64]], axis=1) for h in range(4)]
        res.append([b.astype(BF).reshape(8, 4, 128) for b in both])
    return res


def spread_table():
    row, col = iota((256, 512), 0) % 128, iota((256, 512), 1)
    return one_hot((row % 4 == col // 128) & (row // 4 == col % 32))


def order_table():
    row, col = iota((128, 128), 0), iota((128, 128), 1)
    return one_hot((row % 4 == col // 32) & (row // 4 == col % 32))


def own_modes(r2, spread):
    r2 = r2.reshape(512, 128).astype(F32)
    u = r2[:128] + r2[128:256] + r2[256:384] + r2[384:]
    hi = u.astype(BF)
    lo = (u - hi.astype(F32)).astype(BF)
    return mm(jnp.concatenate([hi, lo], axis=0), spread, TN) * (2.0**-9.5)


def sum_rows(acc):
    row = iota(acc[0].shape, 0)
    half = row < 4
    four = [
        jnp.where(half, acc[k], acc[k + 4]) + pltpu.roll(jnp.where(half, acc[k + 4], acc[k]), 4, 0)
        for k in range(4)
    ]

    def join(a, b, k):
        return jnp.where(row % (2 * k) < k, a + pltpu.roll(a, 8 - k, 0), b + pltpu.roll(b, k, 0))

    return join(join(four[0], four[2], 2), join(four[1], four[3], 2), 1)


def mix_modes(u, w, order):
    blocks = []
    for l in range(2):
        acc = []
        for j in range(4 * l, 4 * l + 4):
            wr, wi = w(2 * j), w(2 * j + 1)
            re = im = None
            for q in range(4):
                ur = jnp.concatenate([u[16 * j : 16 * j + 8, q * 128 : q * 128 + 128]] * 8, axis=1)
                ui = jnp.concatenate([u[16 * j + 8 : 16 * j + 16, q * 128 : q * 128 + 128]] * 8, axis=1)
                r, i = wr[q * 8 : q * 8 + 8], wi[q * 8 : q * 8 + 8]
                a, b = r * ur - i * ui, r * ui + i * ur
                re, im = (a, b) if re is None else (re + a, im + b)
            acc += [re, im]
        y = sum_rows(acc)
        blocks += [y[:, b * 128 : b * 128 + 128] for b in range(8)]
    a = jnp.concatenate(blocks, axis=0).astype(BF)
    return mm(order, a, NT).astype(BF).reshape(32, 4, 128)


def modes_by_kx(r3):
    r3 = r3.reshape(512, 128)
    d = jnp.concatenate(
        [
            jnp.concatenate([r3[h * 128 : h * 128 + 128, l * 64 : l * 64 + 64] for h in range(4)], axis=1)
            for l in range(2)
        ],
        axis=0,
    )
    return jnp.concatenate([d, d], axis=0)


def inverse_xy(d, txi, tyi):
    g = mm(jnp.concatenate(txi, axis=0), d).astype(BF)
    g = [jnp.concatenate([g[k * 64 : k * 64 + 32], g[k * 64 + 32 : k * 64 + 64]], axis=1) for k in range(len(txi))]
    o = mm(jnp.concatenate(g, axis=0), tyi).astype(BF)
    return [
        [o[k * 32 : k * 32 + 32, h * 128 : h * 128 + 128].reshape(2, 4, 4, 128) for h in range(4)]
        for k in range(len(txi))
    ]


def inverse_z(r4, tzi):
    halves = [
        jnp.concatenate([r4[:, o].reshape(128, 128)[:, r * 64 : r * 64 + 64] for o in range(4)], axis=1)
        for r in range(2)
    ]
    res = mm(jnp.concatenate(halves + halves, axis=0), tzi, TN)
    return jnp.transpose(res.reshape(4, 8, 8, 512), (1, 0, 2, 3)).reshape(256, 512)


def gelu(v):
    return 0.5 * v * (1.0 + lax.erf(v * (0.5**0.5)))


def far_first(sizes):
    steps = [()]
    for n in sizes:
        steps = [s + (k,) for s in steps for k in range(n)]
    steps = [s + (c,) for s in steps for c in range(2)]
    steps.sort(key=lambda s: (-sum(min(k, n - k) for k, n in zip(s, sizes)), -s[-1]))
    return steps[:-1]


def kernel(
    x_hbm, diff_hbm, w_hbm, point_hbm, off_hbm, tz_hbm, tx_hbm, ty_hbm, txi_hbm, tyi_hbm, tzi_hbm,
    out_ref,
    x_v, diff_v, w_v, wide_v, spread_v, order_v, point_ref, off_ref, tz_v, tx_v, ty_v, txi_v, tyi_v, tzi_v, pre_v,
    s1, r1, s2, r2, s3, r3, s4, r4, load_sem, send_sem, recv_sem,
):
    g, h = lax.axis_index("gx"), lax.axis_index("gy")
    plane, zz = g // 4, g % 4
    kz = plane * 4 + h
    yy, xc, core = g // 8, (plane % 2) * 2 + h // 2, h % 2
    ys = [lax.rem(yy + k, 4) for k in range(4)]
    zs = [lax.rem(zz + k, 4) for k in range(4)]
    xs = [lax.rem(xc + k, 4) for k in range(4)]
    xhs = [xs[b] // 2 for b in range(4)]
    ups = [[ys[a] * 8 + xhs[b] * 4 for b in range(4)] for a in range(4)]
    gys = [[xs[b] % 2 * 2 + c for c in (core, 1 - core)] for b in range(4)]
    everyone = [(ups[a][b] + zs[c], gys[b][d]) for a, b, c, d in far_first((4, 4, 4))]
    planar = [(ups[a][b], gys[b][d]) for a, b, d in far_first((4, 4))]

    barrier = pltpu.get_barrier_semaphore()
    for peer in everyone:
        pl.semaphore_signal(barrier, inc=1, device_id=peer, device_id_type=MESH)

    loads = [
        (x_hbm, x_v), (tz_hbm, tz_v), (diff_hbm, diff_v), (point_hbm, point_ref), (off_hbm, off_ref), (tx_hbm.at[zz], tx_v), (ty_hbm, ty_v),
        (w_hbm, w_v), (txi_hbm.at[zz], txi_v), (tyi_hbm, tyi_v), (tzi_hbm, tzi_v),
    ]
    loads = [pltpu.make_async_copy(a, b, load_sem.at[k]) for k, (a, b) in enumerate(loads)]
    for c in loads:
        c.start()
    loads[0].wait()
    loads[1].wait()
    xx = cells_by_x(x_v[...]).astype(BF)
    for q, block in enumerate(forward_z(xx, tz_v[...])):
        s1[:, q] = block
    for c in loads[2:5]:
        c.wait()
    diff = diff_v[...].astype(F32)
    pre_v[...] = before_gelu(None, xx, diff, point_ref[...], lambda o: off_ref[o])
    for c in loads[5:]:
        c.wait()
    pl.semaphore_wait(barrier, 127)

    def send(src, dst, phase, peer):
        pltpu.make_async_remote_copy(
            src, dst, send_sem.at[phase], recv_sem.at[phase], device_id=peer, device_id_type=MESH
        ).start()

    def wait(ref, sem):
        pltpu.make_async_copy(ref, ref, sem).wait()

    slot = h * 8 + plane
    for up, gy in planar:
        send(s1.at[up + gy], r1.at[slot], 0, (up + zz, gy))
    r1[slot] = s1[kz]
    spread_v[...] = spread_table()
    order_v[...] = order_table()
    for m in range(16):
        wide_v[m] = w_v[m].astype(F32)
    wait(r1.at[pl.ds(0, 31)], recv_sem.at[0])

    e = forward_y(r1[...], ty_v[...])
    slot = zz * 32 + kz
    for near in ((2, 1), (3, 0)):
        for k, blocks in zip(near, forward_x(e, [tx_v[ys[k]] for k in near])):
            for j, block in enumerate(blocks):
                s2[j, ys[k]] = block
        for a, b, c, d in far_first((4, 4, 4)):
            if a in near:
                up, gy = xhs[b] * 4 + zs[c], gys[b][d]
                send(s2.at[gy, ys[a], up], r2.at[slot], 1, (ys[a] * 8 + up, gy))
    r2[slot] = s2[h, yy, g % 8]
    wait(r2.at[pl.ds(0, 127)], recv_sem.at[1])

    s3[...] = mix_modes(own_modes(r2[...], spread_v[...]), lambda m: wide_v[m], order_v[...])
    slot = h * 32 + g
    for a, b, c, d in far_first((4, 4, 4)):
        up, gy = ups[a][b], gys[b][d]
        send(s3.at[up + gy], r3.at[slot], 2, (up + zs[c], gy))
    r3[slot] = s3[kz]
    wait(r3.at[pl.ds(0, 127)], recv_sem.at[2])

    modes = modes_by_kx(r3[...])
    for near in ((2, 1), (3, 0)):
        for k, blocks in zip(near, inverse_xy(modes, [txi_v[ys[k]] for k in near], tyi_v[...])):
            for j, block in enumerate(blocks):
                s4[ys[k], :, j] = block
        for a, b, d in far_first((4, 4)):
            if a in near:
                send(s4.at[ys[a], xhs[b], gys[b][d]], r4.at[kz], 3, (ups[a][b] + zz, gys[b][d]))
    r4[kz] = s4[yy, plane % 2, h]
    wait(r1.at[pl.ds(0, 31)], recv_sem.at[3])

    act = gelu(pre_v[...] + inverse_z(r4[...], tzi_v[...]))
    act = jnp.stack([act[:, k * 128 : k * 128 + 128].reshape(32, 8, 128) for k in range(4)], axis=1)
    out_ref[...] = act.reshape(1024, 128).astype(BF)

    wait(s1.at[pl.ds(0, 31)], send_sem.at[0])
    wait(r2.at[pl.ds(0, 127)], send_sem.at[1])
    wait(r2.at[pl.ds(0, 127)], send_sem.at[2])
    wait(s1.at[pl.ds(0, 31)], send_sem.at[3])


def on_device(inputs, diffusion, spectral, pointwise, offsets):
    hbm = pl.BlockSpec(memory_space=pltpu.HBM)
    vmem = pl.BlockSpec(memory_space=pltpu.VMEM)
    v = pltpu.VMEM
    args = [inputs.reshape(1024, 128), diffusion, spectral.reshape(16, 32, 1024), pointwise, offsets, *tables()]
    out = pl.pallas_call(
        kernel,
        out_shape=jax.ShapeDtypeStruct((1024, 128), BF),
        in_specs=[hbm] * 11,
        out_specs=vmem,
        scratch_shapes=[
            v((1024, 128), BF), v((4, 8, 128), BF), v((16, 32, 1024), BF), v((16, 32, 1024), F32), v((256, 512), BF), v((128, 128), BF), v((32, 32), BF), pltpu.SMEM((32,), F32),
            v((256, 512), BF), v((4, 64, 768), BF), v((512, 512), BF),
            v((4, 64, 512), BF), v((512, 512), BF), v((512, 512), BF), v((256, 512), F32),
            v((32, 4, 4, 128), BF), v((32, 4, 4, 128), BF),
            v((4, 4, 8, 4, 128), BF), v((128, 4, 128), BF),
            v((32, 4, 128), BF), v((128, 4, 128), BF),
            v((4, 2, 4, 4, 4, 128), BF), v((32, 4, 4, 128), BF),
            pltpu.SemaphoreType.DMA((11,)), pltpu.SemaphoreType.DMA((4,)), pltpu.SemaphoreType.DMA((4,)),
        ],
        compiler_params=pltpu.CompilerParams(
            collective_id=0, has_side_effects=True, vmem_limit_bytes=40 << 20
        ),
    )(*[pltpu.with_memory_space_constraint(a, pltpu.HBM) for a in args])
    return out.reshape(32, 4, 8, 128)


def solution(mesh):
    return jax.shard_map(
        on_device,
        mesh=mesh,
        in_specs=(P(None, "gx", "gy", None), P("gx", "gy", None), P("gx", "gy", None, None, None), P(), P()),
        out_specs=P(None, "gx", "gy", None),
        check_vma=False,
    )
```

```python
import functools

import jax
import jax.numpy as jnp
import ml_dtypes
import numpy as np
from jax import lax
from jax.experimental import pallas as pl
from jax.experimental.pallas import tpu as pltpu
from jax.sharding import PartitionSpec as P

MESH = pl.DeviceIdType.MESH
BF = jnp.bfloat16
F32 = jnp.float32

NT = (((1,), (1,)), ((), ()))
TN = (((0,), (0,)), ((), ()))
NN = (((1,), (0,)), ((), ()))


def mm(a, b, dims=NN):
    return lax.dot_general(a, b, dims, preferred_element_type=F32)


def freq(n):
    j = np.arange(n)
    return np.where(j < n // 2, j, j - n)


def turn(a, b, n):
    return 2.0 * np.pi / n * ((a * b) % n)


def parts(z):
    return np.stack([z.real, z.imag])


def two_parts(t, axis, order):
    high = np.asarray(t, np.float32).astype(ml_dtypes.bfloat16).astype(np.float64)
    return np.concatenate([(high, t - high)[k] for k in order], axis=axis)


def tables():
    eye4, eye8 = np.eye(4), np.eye(8)
    z, kz = np.arange(128), np.arange(32)
    a = parts(np.exp(-1j * turn(kz[:, None], z[None, :], 128)))
    tz = np.einsum("rkz,xw->rkxwz", a, eye4).reshape(256, 512)
    unit = np.array([1.0, 1j])
    y = np.arange(32).reshape(4, 8)
    ky = freq(16).reshape(4, 4)
    ph = turn(y[:, :, None, None], ky[None, None], 32)
    co = np.einsum("hyHk,s,r->hyHksr", np.exp(-1j * ph), np.conj(unit), unit)
    ty = np.einsum("qhyHksr,cd->hrcysHkqd", parts(co), eye8).reshape(512, 512)
    x = 4 * (4 * np.arange(8)[None, :, None] + np.arange(4)[:, None, None]) + np.arange(4)
    kx = np.transpose(freq(64).reshape(4, 8, 2), (0, 2, 1))
    th = turn(kx[None, None, None], x[:, :, :, None, None, None], 128)
    cs = np.stack([np.cos(th), np.sin(th)])
    tx = np.einsum("sZYxylg,cd->ZylgcsYdx", cs, eye4).reshape(4, 4, 64, 256)
    cs = cs.reshape(2, 4, 4, 2, 4, 4, 2, 8)
    txi = np.einsum("sZYhxylg,cd->ZYshcxlygd", cs, eye4).reshape(4, 4, 64, 256)
    co = np.einsum("HyhK,s,r->HyhKsr", np.exp(1j * ph), unit, unit)
    tyi = np.einsum("qHyhKsr,bd->shbKrHqdy", parts(co), eye8).reshape(512, 512)
    b = np.exp(1j * turn(kz[:, None], z[None, :], 128)) * 2.0**-7.5
    tzi = np.einsum("rkz,xw->rkxwz", np.stack([b.real, -b.imag]), eye4).reshape(256, 512)
    tx, txi = two_parts(tx, 3, (0, 1, 0)), two_parts(txi, 3, (0, 1))
    tzi = two_parts(tzi, 0, (0, 1))
    return [jnp.asarray(np.asarray(t, np.float32).astype(ml_dtypes.bfloat16)) for t in (tz, tx, ty, txi, tyi, tzi)]


def iota(shape, dim):
    return lax.broadcasted_iota(jnp.int32, shape, dim)


def one_hot(cond):
    return jnp.where(cond, 1.0, 0.0).astype(BF)


def cells_by_x(x):
    wide = x.astype(F32).reshape(32, 4, 8, 128)
    return jnp.concatenate([wide[:, k].reshape(256, 128) for k in range(4)], axis=1)


def forward_z(xx, tz):
    out = mm(tz, xx, NT)
    res = []
    for q in range(4):
        lanes = slice(q * 64, q * 64 + 64)
        both = jnp.concatenate([out[:128, lanes], out[128:, lanes]], axis=1)
        res.append(both.astype(BF).reshape(32, 4, 128))
    return res


def before_gelu(wide, xx, diff, point, offset):
    rep = one_hot(iota((256, 32), 0) // 8 == iota((256, 32), 1))
    spread = mm(mm(rep, point).astype(BF), rep, NT)
    same_y = iota((256, 256), 0) % 8 == iota((256, 256), 1) % 8
    kron = jnp.where(same_y, spread, 0.0).astype(BF)
    mix = mm(kron, xx)
    gap = iota((128, 128), 0) - iota((128, 128), 1)
    sten = jnp.where(gap == 0, -2.0, jnp.where((gap == 1) | (gap == -1), 1.0, 0.0)).astype(BF)
    cols = []
    for k in range(4):
        lanes = slice(k * 128, k * 128 + 128)
        curv = mm(xx[:, lanes], sten).reshape(32, 8, 128)
        cols.append((curv * diff[k][None]).reshape(256, 128))
    shift = jnp.concatenate([jnp.full((8, 512), offset(o), F32) for o in range(32)], axis=0)
    return mix + jnp.concatenate(cols, axis=1) + shift


def forward_y(r1, ty):
    r1 = r1.reshape(512, 128)
    d = jnp.concatenate([r1[h * 128 : h * 128 + 128] for h in range(4)], axis=1)
    e = mm(d, ty)
    e = jnp.concatenate([e[:, :256], e[:, 256:]], axis=0)
    high = e.astype(BF)
    return jnp.concatenate([high, high, (e - high.astype(F32)).astype(BF)], axis=0)


def forward_x(e, tx):
    o = mm(jnp.concatenate(tx, axis=0), e)
    res = []
    for k in range(len(tx)):
        lo, hi = o[k * 64 : k * 64 + 32], o[k * 64 + 32 : k * 64 + 64]
        both = [jnp.concatenate([lo[:, h * 64 : h * 64 + 64], hi[:, h * 64 : h * 64 + 64]], axis=1) for h in range(4)]
        res.append([b.astype(BF).reshape(8, 4, 128) for b in both])
    return res


def spread_table():
    row, col = iota((256, 512), 0) % 128, iota((256, 512), 1)
    return one_hot((row % 4 == col // 128) & (row // 4 == col % 32))


def order_table():
    row, col = iota((128, 128), 0), iota((128, 128), 1)
    return one_hot((row % 4 == col // 32) & (row // 4 == col % 32))


def own_modes(r2, spread):
    r2 = r2.reshape(512, 128).astype(F32)
    u = r2[:128] + r2[128:256] + r2[256:384] + r2[384:]
    hi = u.astype(BF)
    lo = (u - hi.astype(F32)).astype(BF)
    return mm(jnp.concatenate([hi, lo], axis=0), spread, TN) * (2.0**-9.5)


def sum_rows(acc):
    row = iota(acc[0].shape, 0)
    half = row < 4
    four = [
        jnp.where(half, acc[k], acc[k + 4]) + pltpu.roll(jnp.where(half, acc[k + 4], acc[k]), 4, 0)
        for k in range(4)
    ]

    def join(a, b, k):
        return jnp.where(row % (2 * k) < k, a + pltpu.roll(a, 8 - k, 0), b + pltpu.roll(b, k, 0))

    return join(join(four[0], four[2], 2), join(four[1], four[3], 2), 1)


def mix_modes(u, w, both, order):
    blocks = []
    for l in range(2):
        acc = []
        for j in range(4 * l, 4 * l + 4):
            wr, wi, ws = w(2 * j), w(2 * j + 1), both(j)
            total = None
            for q in range(4):
                ur = jnp.concatenate([u[16 * j : 16 * j + 8, q * 128 : q * 128 + 128]] * 8, axis=1)
                ui = jnp.concatenate([u[16 * j + 8 : 16 * j + 16, q * 128 : q * 128 + 128]] * 8, axis=1)
                r, i = wr[q * 8 : q * 8 + 8], wi[q * 8 : q * 8 + 8]
                p = ws[q * 8 : q * 8 + 8] * ur, r * (ui - ur), i * (ur + ui)
                total = p if total is None else [a + b for a, b in zip(total, p)]
            acc += [total[0] - total[2], total[0] + total[1]]
        y = sum_rows(acc)
        blocks += [y[:, b * 128 : b * 128 + 128] for b in range(8)]
    a = jnp.concatenate(blocks, axis=0).astype(BF)
    return mm(order, a, NT).astype(BF).reshape(32, 4, 128)


def modes_by_kx(r3):
    r3 = r3.reshape(512, 128)
    d = jnp.concatenate(
        [
            jnp.concatenate([r3[h * 128 : h * 128 + 128, l * 64 : l * 64 + 64] for h in range(4)], axis=1)
            for l in range(2)
        ],
        axis=0,
    )
    return jnp.concatenate([d, d], axis=0)


def inverse_xy(d, txi, tyi):
    g = mm(jnp.concatenate(txi, axis=0), d).astype(BF)
    g = [jnp.concatenate([g[k * 64 : k * 64 + 32], g[k * 64 + 32 : k * 64 + 64]], axis=1) for k in range(len(txi))]
    o = mm(jnp.concatenate(g, axis=0), tyi).astype(BF)
    return [
        [o[k * 32 : k * 32 + 32, h * 128 : h * 128 + 128].reshape(2, 4, 4, 128) for h in range(4)]
        for k in range(len(txi))
    ]


def inverse_z(r4, tzi):
    halves = [
        jnp.concatenate([r4[:, o].reshape(128, 128)[:, r * 64 : r * 64 + 64] for o in range(4)], axis=1)
        for r in range(2)
    ]
    res = mm(jnp.concatenate(halves + halves, axis=0), tzi, TN)
    return jnp.transpose(res.reshape(4, 8, 8, 512), (1, 0, 2, 3)).reshape(256, 512)


def gelu(v):
    return 0.5 * v * (1.0 + lax.erf(v * (0.5**0.5)))


def far_first(sizes):
    steps = [()]
    for n in sizes:
        steps = [s + (k,) for s in steps for k in range(n)]
    steps = [s + (c,) for s in steps for c in range(2)]
    steps.sort(key=lambda s: (-sum(min(k, n - k) for k, n in zip(s, sizes)), -s[-1]))
    return steps[:-1]


def kernel(
    x_hbm, diff_hbm, w_hbm, point_hbm, off_hbm, tz_hbm, tx_hbm, ty_hbm, txi_hbm, tyi_hbm, tzi_hbm,
    out_ref,
    x_v, diff_v, w_v, wide_v, both_v, spread_v, order_v, point_ref, off_ref, tz_v, tx_v, ty_v, txi_v, tyi_v, tzi_v, pre_v,
    s1, r1, s2, r2, s3, r3, s4, r4, load_sem, send_sem, recv_sem,
):
    g, h = lax.axis_index("gx"), lax.axis_index("gy")
    plane, zz = g // 4, g % 4
    kz = plane * 4 + h
    yy, xc, core = g // 8, (plane % 2) * 2 + h // 2, h % 2
    ys = [lax.rem(yy + k, 4) for k in range(4)]
    zs = [lax.rem(zz + k, 4) for k in range(4)]
    xs = [lax.rem(xc + k, 4) for k in range(4)]
    xhs = [xs[b] // 2 for b in range(4)]
    ups = [[ys[a] * 8 + xhs[b] * 4 for b in range(4)] for a in range(4)]
    gys = [[xs[b] % 2 * 2 + c for c in (core, 1 - core)] for b in range(4)]
    everyone = [(ups[a][b] + zs[c], gys[b][d]) for a, b, c, d in far_first((4, 4, 4))]
    planar = [(ups[a][b], gys[b][d]) for a, b, d in far_first((4, 4))]

    barrier = pltpu.get_barrier_semaphore()
    for peer in everyone:
        pl.semaphore_signal(barrier, inc=1, device_id=peer, device_id_type=MESH)

    loads = [
        (x_hbm, x_v), (tz_hbm, tz_v), (diff_hbm, diff_v), (point_hbm, point_ref), (off_hbm, off_ref), (tx_hbm.at[zz], tx_v), (ty_hbm, ty_v),
        (w_hbm, w_v), (txi_hbm.at[zz], txi_v), (tyi_hbm, tyi_v), (tzi_hbm, tzi_v),
    ]
    loads = [pltpu.make_async_copy(a, b, load_sem.at[k]) for k, (a, b) in enumerate(loads)]
    for c in loads:
        c.start()
    loads[0].wait()
    loads[1].wait()
    xx = cells_by_x(x_v[...]).astype(BF)
    for q, block in enumerate(forward_z(xx, tz_v[...])):
        s1[:, q] = block
    for c in loads[2:5]:
        c.wait()
    diff = diff_v[...].astype(F32)
    pre_v[...] = before_gelu(None, xx, diff, point_ref[...], lambda o: off_ref[o])
    for c in loads[5:]:
        c.wait()
    pl.semaphore_wait(barrier, 127)

    def send(src, dst, phase, peer):
        pltpu.make_async_remote_copy(
            src, dst, send_sem.at[phase], recv_sem.at[phase], device_id=peer, device_id_type=MESH
        ).start()

    def wait(ref, sem):
        pltpu.make_async_copy(ref, ref, sem).wait()

    slot = h * 8 + plane
    for up, gy in planar:
        send(s1.at[up + gy], r1.at[slot], 0, (up + zz, gy))
    r1[slot] = s1[kz]
    spread_v[...] = spread_table()
    order_v[...] = order_table()
    for m in range(16):
        wide_v[m] = w_v[m].astype(F32)
    for j in range(8):
        both_v[j] = wide_v[2 * j] + wide_v[2 * j + 1]
    wait(r1.at[pl.ds(0, 31)], recv_sem.at[0])

    e = forward_y(r1[...], ty_v[...])
    slot = zz * 32 + kz
    for near in ((2, 1), (3, 0)):
        for k, blocks in zip(near, forward_x(e, [tx_v[ys[k]] for k in near])):
            for j, block in enumerate(blocks):
                s2[j, ys[k]] = block
        for a, b, c, d in far_first((4, 4, 4)):
            if a in near:
                up, gy = xhs[b] * 4 + zs[c], gys[b][d]
                send(s2.at[gy, ys[a], up], r2.at[slot], 1, (ys[a] * 8 + up, gy))
    r2[slot] = s2[h, yy, g % 8]
    wait(r2.at[pl.ds(0, 127)], recv_sem.at[1])

    s3[...] = mix_modes(own_modes(r2[...], spread_v[...]), lambda m: wide_v[m], lambda j: both_v[j], order_v[...])
    slot = h * 32 + g
    for a, b, c, d in far_first((4, 4, 4)):
        up, gy = ups[a][b], gys[b][d]
        send(s3.at[up + gy], r3.at[slot], 2, (up + zs[c], gy))
    r3[slot] = s3[kz]
    wait(r3.at[pl.ds(0, 127)], recv_sem.at[2])

    modes = modes_by_kx(r3[...])
    for near in ((2, 1), (3, 0)):
        for k, blocks in zip(near, inverse_xy(modes, [txi_v[ys[k]] for k in near], tyi_v[...])):
            for j, block in enumerate(blocks):
                s4[ys[k], :, j] = block
        for a, b, d in far_first((4, 4)):
            if a in near:
                send(s4.at[ys[a], xhs[b], gys[b][d]], r4.at[kz], 3, (ups[a][b] + zz, gys[b][d]))
    r4[kz] = s4[yy, plane % 2, h]
    wait(r1.at[pl.ds(0, 31)], recv_sem.at[3])

    act = gelu(pre_v[...] + inverse_z(r4[...], tzi_v[...]))
    act = jnp.stack([act[:, k * 128 : k * 128 + 128].reshape(32, 8, 128) for k in range(4)], axis=1)
    out_ref[...] = act.reshape(1024, 128).astype(BF)

    wait(s1.at[pl.ds(0, 31)], send_sem.at[0])
    wait(r2.at[pl.ds(0, 127)], send_sem.at[1])
    wait(r2.at[pl.ds(0, 127)], send_sem.at[2])
    wait(s1.at[pl.ds(0, 31)], send_sem.at[3])


def on_device(inputs, diffusion, spectral, pointwise, offsets):
    hbm = pl.BlockSpec(memory_space=pltpu.HBM)
    vmem = pl.BlockSpec(memory_space=pltpu.VMEM)
    v = pltpu.VMEM
    args = [inputs.reshape(1024, 128), diffusion, spectral.reshape(16, 32, 1024), pointwise, offsets, *tables()]
    out = pl.pallas_call(
        kernel,
        out_shape=jax.ShapeDtypeStruct((1024, 128), BF),
        in_specs=[hbm] * 11,
        out_specs=vmem,
        scratch_shapes=[
            v((1024, 128), BF), v((4, 8, 128), BF), v((16, 32, 1024), BF), v((16, 32, 1024), F32), v((8, 32, 1024), F32), v((256, 512), BF), v((128, 128), BF), v((32, 32), BF), pltpu.SMEM((32,), F32),
            v((256, 512), BF), v((4, 64, 768), BF), v((512, 512), BF),
            v((4, 64, 512), BF), v((512, 512), BF), v((512, 512), BF), v((256, 512), F32),
            v((32, 4, 4, 128), BF), v((32, 4, 4, 128), BF),
            v((4, 4, 8, 4, 128), BF), v((128, 4, 128), BF),
            v((32, 4, 128), BF), v((128, 4, 128), BF),
            v((4, 2, 4, 4, 4, 128), BF), v((32, 4, 4, 128), BF),
            pltpu.SemaphoreType.DMA((11,)), pltpu.SemaphoreType.DMA((4,)), pltpu.SemaphoreType.DMA((4,)),
        ],
        compiler_params=pltpu.CompilerParams(
            collective_id=0, has_side_effects=True, vmem_limit_bytes=40 << 20
        ),
    )(*[pltpu.with_memory_space_constraint(a, pltpu.HBM) for a in args])
    return out.reshape(32, 4, 8, 128)


def solution(mesh):
    return jax.shard_map(
        on_device,
        mesh=mesh,
        in_specs=(P(None, "gx", "gy", None), P("gx", "gy", None), P("gx", "gy", None, None, None), P(), P()),
        out_specs=P(None, "gx", "gy", None),
        check_vma=False,
    )
```

```python
import functools

import jax
import jax.numpy as jnp
import ml_dtypes
import numpy as np
from jax import lax
from jax.experimental import pallas as pl
from jax.experimental.pallas import tpu as pltpu
from jax.sharding import PartitionSpec as P

MESH = pl.DeviceIdType.MESH
BF = jnp.bfloat16
F32 = jnp.float32

NT = (((1,), (1,)), ((), ()))
TN = (((0,), (0,)), ((), ()))
NN = (((1,), (0,)), ((), ()))


def mm(a, b, dims=NN):
    return lax.dot_general(a, b, dims, preferred_element_type=F32)


def freq(n):
    j = np.arange(n)
    return np.where(j < n // 2, j, j - n)


def turn(a, b, n):
    return 2.0 * np.pi / n * ((a * b) % n)


def parts(z):
    return np.stack([z.real, z.imag])


def two_parts(t, axis, order):
    high = np.asarray(t, np.float32).astype(ml_dtypes.bfloat16).astype(np.float64)
    return np.concatenate([(high, t - high)[k] for k in order], axis=axis)


def tables():
    eye4, eye8 = np.eye(4), np.eye(8)
    z, kz = np.arange(128), np.arange(32)
    a = parts(np.exp(-1j * turn(kz[:, None], z[None, :], 128)))
    tz = np.einsum("rkz,xw->rkxwz", a, eye4).reshape(256, 512)
    unit = np.array([1.0, 1j])
    y = np.arange(32).reshape(4, 8)
    ky = freq(16).reshape(4, 4)
    ph = turn(y[:, :, None, None], ky[None, None], 32)
    co = np.einsum("hyHk,s,r->hyHksr", np.exp(-1j * ph), np.conj(unit), unit)
    ty = np.einsum("qhyHksr,cd->hrcysHkqd", parts(co), eye8).reshape(512, 512)
    x = 4 * (4 * np.arange(8)[None, :, None] + np.arange(4)[:, None, None]) + np.arange(4)
    kx = np.transpose(freq(64).reshape(4, 8, 2), (0, 2, 1))
    th = turn(kx[None, None, None], x[:, :, :, None, None, None], 128)
    cs = np.stack([np.cos(th), np.sin(th)])
    tx = np.einsum("sZYxylg,cd->ZylgcsYdx", cs, eye4).reshape(4, 4, 64, 256)
    cs = cs.reshape(2, 4, 4, 2, 4, 4, 2, 8)
    txi = np.einsum("sZYhxylg,cd->ZYshcxlygd", cs, eye4).reshape(4, 4, 64, 256)
    co = np.einsum("HyhK,s,r->HyhKsr", np.exp(1j * ph), unit, unit)
    tyi = np.einsum("qHyhKsr,bd->shbKrHqdy", parts(co), eye8).reshape(512, 512)
    b = np.exp(1j * turn(kz[:, None], z[None, :], 128)) * 2.0**-7.5
    tzi = np.einsum("rkz,xw->rkxwz", np.stack([b.real, -b.imag]), eye4).reshape(256, 512)
    tx, txi = two_parts(tx, 3, (0, 1, 0)), two_parts(txi, 3, (0, 1))
    tzi = two_parts(tzi, 0, (0, 1))
    return [jnp.asarray(np.asarray(t, np.float32).astype(ml_dtypes.bfloat16)) for t in (tz, tx, ty, txi, tyi, tzi)]


def iota(shape, dim):
    return lax.broadcasted_iota(jnp.int32, shape, dim)


def one_hot(cond):
    return jnp.where(cond, 1.0, 0.0).astype(BF)


def cells_by_x(x):
    wide = x.astype(F32).reshape(32, 4, 8, 128)
    return jnp.concatenate([wide[:, k].reshape(256, 128) for k in range(4)], axis=1)


def forward_z(xx, tz):
    out = mm(tz, xx, NT)
    res = []
    for q in range(4):
        lanes = slice(q * 64, q * 64 + 64)
        both = jnp.concatenate([out[:128, lanes], out[128:, lanes]], axis=1)
        res.append(both.astype(BF).reshape(32, 4, 128))
    return res


def before_gelu(wide, xx, diff, point, offset):
    rep = one_hot(iota((256, 32), 0) // 8 == iota((256, 32), 1))
    spread = mm(mm(rep, point).astype(BF), rep, NT)
    same_y = iota((256, 256), 0) % 8 == iota((256, 256), 1) % 8
    kron = jnp.where(same_y, spread, 0.0).astype(BF)
    mix = mm(kron, xx)
    gap = iota((128, 128), 0) - iota((128, 128), 1)
    sten = jnp.where(gap == 0, -2.0, jnp.where((gap == 1) | (gap == -1), 1.0, 0.0)).astype(BF)
    cols = []
    for k in range(4):
        lanes = slice(k * 128, k * 128 + 128)
        curv = mm(xx[:, lanes], sten).reshape(32, 8, 128)
        cols.append((curv * diff[k][None]).reshape(256, 128))
    shift = jnp.concatenate([jnp.full((8, 512), offset(o), F32) for o in range(32)], axis=0)
    return mix + jnp.concatenate(cols, axis=1) + shift


def forward_y(r1, ty):
    r1 = r1.reshape(512, 128)
    d = jnp.concatenate([r1[h * 128 : h * 128 + 128] for h in range(4)], axis=1)
    e = mm(d, ty)
    e = jnp.concatenate([e[:, :256], e[:, 256:]], axis=0)
    high = e.astype(BF)
    return jnp.concatenate([high, high, (e - high.astype(F32)).astype(BF)], axis=0)


def forward_x(e, tx):
    o = mm(jnp.concatenate(tx, axis=0), e)
    res = []
    for k in range(len(tx)):
        lo, hi = o[k * 64 : k * 64 + 32], o[k * 64 + 32 : k * 64 + 64]
        both = [jnp.concatenate([lo[:, h * 64 : h * 64 + 64], hi[:, h * 64 : h * 64 + 64]], axis=1) for h in range(4)]
        res.append([b.astype(BF).reshape(8, 4, 128) for b in both])
    return res


def spread_table():
    row, col = iota((256, 512), 0) % 128, iota((256, 512), 1)
    return one_hot((row % 4 == col // 128) & (row // 4 == col % 32))


def order_table():
    row, col = iota((128, 128), 0), iota((128, 128), 1)
    return one_hot((row % 4 == col // 32) & (row // 4 == col % 32))


def own_modes(r2, spread):
    r2 = r2.reshape(512, 128).astype(F32)
    u = r2[:128] + r2[128:256] + r2[256:384] + r2[384:]
    hi = u.astype(BF)
    lo = (u - hi.astype(F32)).astype(BF)
    return mm(jnp.concatenate([hi, lo], axis=0), spread, TN) * (2.0**-9.5)


def sum_rows(acc):
    row = iota(acc[0].shape, 0)
    half = row < 4
    four = [
        jnp.where(half, acc[k], acc[k + 4]) + pltpu.roll(jnp.where(half, acc[k + 4], acc[k]), 4, 0)
        for k in range(4)
    ]

    def join(a, b, k):
        return jnp.where(row % (2 * k) < k, a + pltpu.roll(a, 8 - k, 0), b + pltpu.roll(b, k, 0))

    return join(join(four[0], four[2], 2), join(four[1], four[3], 2), 1)


def mix_modes(u, w, order):
    blocks = []
    for l in range(2):
        acc = []
        for j in range(4 * l, 4 * l + 4):
            wr, wi = w(2 * j), w(2 * j + 1)
            re = im = None
            for q in range(4):
                ur = jnp.concatenate([u[16 * j : 16 * j + 8, q * 128 : q * 128 + 128]] * 8, axis=1)
                ui = jnp.concatenate([u[16 * j + 8 : 16 * j + 16, q * 128 : q * 128 + 128]] * 8, axis=1)
                r, i = wr[q * 8 : q * 8 + 8], wi[q * 8 : q * 8 + 8]
                a, b = r * ur - i * ui, r * ui + i * ur
                re, im = (a, b) if re is None else (re + a, im + b)
            acc += [re, im]
        y = sum_rows(acc)
        blocks += [y[:, b * 128 : b * 128 + 128] for b in range(8)]
    a = jnp.concatenate(blocks, axis=0).astype(BF)
    return mm(order, a, NT).astype(BF).reshape(32, 4, 128)


def modes_by_kx(r3):
    r3 = r3.reshape(512, 128)
    d = jnp.concatenate(
        [
            jnp.concatenate([r3[h * 128 : h * 128 + 128, l * 64 : l * 64 + 64] for h in range(4)], axis=1)
            for l in range(2)
        ],
        axis=0,
    )
    return jnp.concatenate([d, d], axis=0)


def inverse_xy(d, txi, tyi):
    g = mm(jnp.concatenate(txi, axis=0), d).astype(BF)
    g = [jnp.concatenate([g[k * 64 : k * 64 + 32], g[k * 64 + 32 : k * 64 + 64]], axis=1) for k in range(len(txi))]
    o = mm(jnp.concatenate(g, axis=0), tyi).astype(BF)
    return [
        [o[k * 32 : k * 32 + 32, h * 128 : h * 128 + 128].reshape(2, 4, 4, 128) for h in range(4)]
        for k in range(len(txi))
    ]


def inverse_z(r4, tzi):
    halves = [
        jnp.concatenate([r4[:, o].reshape(128, 128)[:, r * 64 : r * 64 + 64] for o in range(4)], axis=1)
        for r in range(2)
    ]
    res = mm(jnp.concatenate(halves + halves, axis=0), tzi, TN)
    return jnp.transpose(res.reshape(4, 8, 8, 512), (1, 0, 2, 3)).reshape(256, 512)


def gelu(v):
    return 0.5 * v * (1.0 + lax.erf(v * (0.5**0.5)))


def far_first(sizes):
    steps = [()]
    for n in sizes:
        steps = [s + (k,) for s in steps for k in range(n)]
    steps = [s + (c,) for s in steps for c in range(2)]
    steps.sort(key=lambda s: (-sum(min(k, n - k) for k, n in zip(s, sizes)), -s[-1]))
    return steps[:-1]


def kernel(
    x_hbm, diff_hbm, w_hbm, point_hbm, off_hbm, tz_hbm, tx_hbm, ty_hbm, txi_hbm, tyi_hbm, tzi_hbm,
    out_ref,
    x_v, diff_v, w_v, wide_v, spread_v, order_v, point_ref, off_ref, tz_v, tx_v, ty_v, txi_v, tyi_v, tzi_v, pre_v,
    s1, r1, s2, r2, s3, r3, s4, r4, load_sem, send_sem, recv_sem,
):
    g, h = lax.axis_index("gx"), lax.axis_index("gy")
    plane, zz = g // 4, g % 4
    kz = plane * 4 + h
    yy, xc, core = g // 8, (plane % 2) * 2 + h // 2, h % 2
    ys = [lax.rem(yy + k, 4) for k in range(4)]
    zs = [lax.rem(zz + k, 4) for k in range(4)]
    xs = [lax.rem(xc + k, 4) for k in range(4)]
    xhs = [xs[b] // 2 for b in range(4)]
    ups = [[ys[a] * 8 + xhs[b] * 4 for b in range(4)] for a in range(4)]
    gys = [[xs[b] % 2 * 2 + c for c in (core, 1 - core)] for b in range(4)]
    everyone = [(ups[a][b] + zs[c], gys[b][d]) for a, b, c, d in far_first((4, 4, 4))]
    planar = [(ups[a][b], gys[b][d]) for a, b, d in far_first((4, 4))]

    barrier = pltpu.get_barrier_semaphore()
    for peer in everyone:
        pl.semaphore_signal(barrier, inc=1, device_id=peer, device_id_type=MESH)

    loads = [
        (x_hbm, x_v), (tz_hbm, tz_v), (diff_hbm, diff_v), (point_hbm, point_ref), (off_hbm, off_ref), (tx_hbm.at[zz], tx_v), (ty_hbm, ty_v),
        (w_hbm, w_v), (txi_hbm.at[zz], txi_v), (tyi_hbm, tyi_v), (tzi_hbm, tzi_v),
    ]
    loads = [pltpu.make_async_copy(a, b, load_sem.at[k]) for k, (a, b) in enumerate(loads)]
    for c in loads:
        c.start()
    loads[0].wait()
    loads[1].wait()
    xx = cells_by_x(x_v[...]).astype(BF)
    for q, block in enumerate(forward_z(xx, tz_v[...])):
        s1[:, q] = block
    for c in loads[2:5]:
        c.wait()
    diff = diff_v[...].astype(F32)
    pre_v[...] = before_gelu(None, xx, diff, point_ref[...], lambda o: off_ref[o])
    for c in loads[5:]:
        c.wait()
    pl.semaphore_wait(barrier, 127)

    def send(src, dst, phase, peer):
        pltpu.make_async_remote_copy(
            src, dst, send_sem.at[phase], recv_sem.at[phase], device_id=peer, device_id_type=MESH
        ).start()

    def wait(ref, sem):
        pltpu.make_async_copy(ref, ref, sem).wait()

    slot = h * 8 + plane
    for up, gy in planar:
        send(s1.at[up + gy], r1.at[slot], 0, (up + zz, gy))
    r1[slot] = s1[kz]
    spread_v[...] = spread_table()
    order_v[...] = order_table()
    for m in range(16):
        wide_v[m] = w_v[m].astype(F32)
    wait(r1.at[pl.ds(0, 31)], recv_sem.at[0])

    e = forward_y(r1[...], ty_v[...])
    slot = zz * 32 + kz
    for near in ((2, 1, 3, 0),):
        for k, blocks in zip(near, forward_x(e, [tx_v[ys[k]] for k in near])):
            for j, block in enumerate(blocks):
                s2[j, ys[k]] = block
        for a, b, c, d in far_first((4, 4, 4)):
            if a in near:
                up, gy = xhs[b] * 4 + zs[c], gys[b][d]
                send(s2.at[gy, ys[a], up], r2.at[slot], 1, (ys[a] * 8 + up, gy))
    r2[slot] = s2[h, yy, g % 8]
    wait(r2.at[pl.ds(0, 127)], recv_sem.at[1])

    s3[...] = mix_modes(own_modes(r2[...], spread_v[...]), lambda m: wide_v[m], order_v[...])
    slot = h * 32 + g
    for a, b, c, d in far_first((4, 4, 4)):
        up, gy = ups[a][b], gys[b][d]
        send(s3.at[up + gy], r3.at[slot], 2, (up + zs[c], gy))
    r3[slot] = s3[kz]
    wait(r3.at[pl.ds(0, 127)], recv_sem.at[2])

    modes = modes_by_kx(r3[...])
    for near in ((2, 1, 3, 0),):
        for k, blocks in zip(near, inverse_xy(modes, [txi_v[ys[k]] for k in near], tyi_v[...])):
            for j, block in enumerate(blocks):
                s4[ys[k], :, j] = block
        for a, b, d in far_first((4, 4)):
            if a in near:
                send(s4.at[ys[a], xhs[b], gys[b][d]], r4.at[kz], 3, (ups[a][b] + zz, gys[b][d]))
    r4[kz] = s4[yy, plane % 2, h]
    wait(r1.at[pl.ds(0, 31)], recv_sem.at[3])

    act = gelu(pre_v[...] + inverse_z(r4[...], tzi_v[...]))
    act = jnp.stack([act[:, k * 128 : k * 128 + 128].reshape(32, 8, 128) for k in range(4)], axis=1)
    out_ref[...] = act.reshape(1024, 128).astype(BF)

    wait(s1.at[pl.ds(0, 31)], send_sem.at[0])
    wait(r2.at[pl.ds(0, 127)], send_sem.at[1])
    wait(r2.at[pl.ds(0, 127)], send_sem.at[2])
    wait(s1.at[pl.ds(0, 31)], send_sem.at[3])


def on_device(inputs, diffusion, spectral, pointwise, offsets):
    hbm = pl.BlockSpec(memory_space=pltpu.HBM)
    vmem = pl.BlockSpec(memory_space=pltpu.VMEM)
    v = pltpu.VMEM
    args = [inputs.reshape(1024, 128), diffusion, spectral.reshape(16, 32, 1024), pointwise, offsets, *tables()]
    out = pl.pallas_call(
        kernel,
        out_shape=jax.ShapeDtypeStruct((1024, 128), BF),
        in_specs=[hbm] * 11,
        out_specs=vmem,
        scratch_shapes=[
            v((1024, 128), BF), v((4, 8, 128), BF), v((16, 32, 1024), BF), v((16, 32, 1024), F32), v((256, 512), BF), v((128, 128), BF), v((32, 32), BF), pltpu.SMEM((32,), F32),
            v((256, 512), BF), v((4, 64, 768), BF), v((512, 512), BF),
            v((4, 64, 512), BF), v((512, 512), BF), v((512, 512), BF), v((256, 512), F32),
            v((32, 4, 4, 128), BF), v((32, 4, 4, 128), BF),
            v((4, 4, 8, 4, 128), BF), v((128, 4, 128), BF),
            v((32, 4, 128), BF), v((128, 4, 128), BF),
            v((4, 2, 4, 4, 4, 128), BF), v((32, 4, 4, 128), BF),
            pltpu.SemaphoreType.DMA((11,)), pltpu.SemaphoreType.DMA((4,)), pltpu.SemaphoreType.DMA((4,)),
        ],
        compiler_params=pltpu.CompilerParams(
            collective_id=0, has_side_effects=True, vmem_limit_bytes=40 << 20
        ),
    )(*[pltpu.with_memory_space_constraint(a, pltpu.HBM) for a in args])
    return out.reshape(32, 4, 8, 128)


def solution(mesh):
    return jax.shard_map(
        on_device,
        mesh=mesh,
        in_specs=(P(None, "gx", "gy", None), P("gx", "gy", None), P("gx", "gy", None, None, None), P(), P()),
        out_specs=P(None, "gx", "gy", None),
        check_vma=False,
    )
```

```python
import functools

import jax
import jax.numpy as jnp
import ml_dtypes
import numpy as np
from jax import lax
from jax.experimental import pallas as pl
from jax.experimental.pallas import tpu as pltpu
from jax.sharding import PartitionSpec as P

MESH = pl.DeviceIdType.MESH
BF = jnp.bfloat16
F32 = jnp.float32

NT = (((1,), (1,)), ((), ()))
TN = (((0,), (0,)), ((), ()))
NN = (((1,), (0,)), ((), ()))


def mm(a, b, dims=NN):
    return lax.dot_general(a, b, dims, preferred_element_type=F32)


def freq(n):
    j = np.arange(n)
    return np.where(j < n // 2, j, j - n)


def turn(a, b, n):
    return 2.0 * np.pi / n * ((a * b) % n)


def parts(z):
    return np.stack([z.real, z.imag])


def two_parts(t, axis, order):
    high = np.asarray(t, np.float32).astype(ml_dtypes.bfloat16).astype(np.float64)
    return np.concatenate([(high, t - high)[k] for k in order], axis=axis)


def tables():
    eye4, eye8 = np.eye(4), np.eye(8)
    z, kz = np.arange(128), np.arange(32)
    a = parts(np.exp(-1j * turn(kz[:, None], z[None, :], 128)))
    tz = np.einsum("rkz,xw->rkxwz", a, eye4).reshape(256, 512)
    unit = np.array([1.0, 1j])
    y = np.arange(32).reshape(4, 8)
    ky = freq(16).reshape(4, 4)
    ph = turn(y[:, :, None, None], ky[None, None], 32)
    co = np.einsum("hyHk,s,r->hyHksr", np.exp(-1j * ph), np.conj(unit), unit)
    ty = np.einsum("qhyHksr,cd->hrcysHkqd", parts(co), eye8).reshape(512, 512)
    x = 4 * (4 * np.arange(8)[None, :, None] + np.arange(4)[:, None, None]) + np.arange(4)
    kx = np.transpose(freq(64).reshape(4, 8, 2), (0, 2, 1))
    th = turn(kx[None, None, None], x[:, :, :, None, None, None], 128)
    cs = np.stack([np.cos(th), np.sin(th)])
    tx = np.einsum("sZYxylg,cd->ZylgcsYdx", cs, eye4).reshape(4, 4, 64, 256)
    cs = cs.reshape(2, 4, 4, 2, 4, 4, 2, 8)
    txi = np.einsum("sZYhxylg,cd->ZYshcxlygd", cs, eye4).reshape(4, 4, 64, 256)
    co = np.einsum("HyhK,s,r->HyhKsr", np.exp(1j * ph), unit, unit)
    tyi = np.einsum("qHyhKsr,bd->shbKrHqdy", parts(co), eye8).reshape(512, 512)
    b = np.exp(1j * turn(kz[:, None], z[None, :], 128)) * 2.0**-7.5
    tzi = np.einsum("rkz,xw->rkxwz", np.stack([b.real, -b.imag]), eye4).reshape(256, 512)
    tx, txi = two_parts(tx, 3, (0, 1, 0)), two_parts(txi, 3, (0, 1))
    return [jnp.asarray(np.asarray(t, np.float32).astype(ml_dtypes.bfloat16)) for t in (tz, tx, ty, txi, tyi, tzi)]


def iota(shape, dim):
    return lax.broadcasted_iota(jnp.int32, shape, dim)


def one_hot(cond):
    return jnp.where(cond, 1.0, 0.0).astype(BF)


def cells_by_x(x):
    wide = x.astype(F32).reshape(32, 4, 8, 128)
    return jnp.concatenate([wide[:, k].reshape(256, 128) for k in range(4)], axis=1)


def forward_z(xx, tz):
    out = mm(tz, xx, NT)
    res = []
    for q in range(4):
        lanes = slice(q * 64, q * 64 + 64)
        both = jnp.concatenate([out[:128, lanes], out[128:, lanes]], axis=1)
        res.append(both.astype(BF).reshape(32, 4, 128))
    return res


def before_gelu(wide, xx, diff, point, offset):
    rep = one_hot(iota((256, 32), 0) // 8 == iota((256, 32), 1))
    spread = mm(mm(rep, point).astype(BF), rep, NT)
    same_y = iota((256, 256), 0) % 8 == iota((256, 256), 1) % 8
    kron = jnp.where(same_y, spread, 0.0).astype(BF)
    mix = mm(kron, xx)
    gap = iota((128, 128), 0) - iota((128, 128), 1)
    sten = jnp.where(gap == 0, -2.0, jnp.where((gap == 1) | (gap == -1), 1.0, 0.0)).astype(BF)
    cols = []
    for k in range(4):
        lanes = slice(k * 128, k * 128 + 128)
        curv = mm(xx[:, lanes], sten).reshape(32, 8, 128)
        cols.append((curv * diff[k][None]).reshape(256, 128))
    shift = jnp.concatenate([jnp.full((8, 512), offset(o), F32) for o in range(32)], axis=0)
    return mix + jnp.concatenate(cols, axis=1) + shift


def forward_y(r1, ty):
    r1 = r1.reshape(512, 128)
    d = jnp.concatenate([r1[h * 128 : h * 128 + 128] for h in range(4)], axis=1)
    e = mm(d, ty)
    e = jnp.concatenate([e[:, :256], e[:, 256:]], axis=0)
    high = e.astype(BF)
    return jnp.concatenate([high, high, (e - high.astype(F32)).astype(BF)], axis=0)


def forward_x(e, tx):
    o = mm(jnp.concatenate(tx, axis=0), e)
    res = []
    for k in range(len(tx)):
        lo, hi = o[k * 64 : k * 64 + 32], o[k * 64 + 32 : k * 64 + 64]
        both = [jnp.concatenate([lo[:, h * 64 : h * 64 + 64], hi[:, h * 64 : h * 64 + 64]], axis=1) for h in range(4)]
        res.append([b.astype(BF).reshape(8, 4, 128) for b in both])
    return res


def spread_table():
    row, col = iota((256, 512), 0) % 128, iota((256, 512), 1)
    return one_hot((row % 4 == col // 128) & (row // 4 == col % 32))


def order_table():
    row, col = iota((128, 128), 0), iota((128, 128), 1)
    return one_hot((row % 4 == col // 32) & (row // 4 == col % 32))


def own_modes(r2, spread):
    r2 = r2.reshape(512, 128).astype(F32)
    u = r2[:128] + r2[128:256] + r2[256:384] + r2[384:]
    hi = u.astype(BF)
    lo = (u - hi.astype(F32)).astype(BF)
    return mm(jnp.concatenate([hi, lo], axis=0), spread, TN) * (2.0**-9.5)


def sum_rows(acc):
    row = iota(acc[0].shape, 0)
    half = row < 4
    four = [
        jnp.where(half, acc[k], acc[k + 4]) + pltpu.roll(jnp.where(half, acc[k + 4], acc[k]), 4, 0)
        for k in range(4)
    ]

    def join(a, b, k):
        return jnp.where(row % (2 * k) < k, a + pltpu.roll(a, 8 - k, 0), b + pltpu.roll(b, k, 0))

    return join(join(four[0], four[2], 2), join(four[1], four[3], 2), 1)


def mix_modes(u, w, order):
    blocks = []
    for l in range(2):
        acc = []
        for j in range(4 * l, 4 * l + 4):
            wr, wi = w(2 * j), w(2 * j + 1)
            re = im = None
            for q in range(4):
                ur = jnp.concatenate([u[16 * j : 16 * j + 8, q * 128 : q * 128 + 128]] * 8, axis=1)
                ui = jnp.concatenate([u[16 * j + 8 : 16 * j + 16, q * 128 : q * 128 + 128]] * 8, axis=1)
                r, i = wr[q * 8 : q * 8 + 8], wi[q * 8 : q * 8 + 8]
                a, b = r * ur - i * ui, r * ui + i * ur
                re, im = (a, b) if re is None else (re + a, im + b)
            acc += [re, im]
        y = sum_rows(acc)
        blocks += [y[:, b * 128 : b * 128 + 128] for b in range(8)]
    a = jnp.concatenate(blocks, axis=0).astype(BF)
    return mm(order, a, NT).astype(BF).reshape(32, 4, 128)


def modes_by_kx(r3):
    r3 = r3.reshape(512, 128)
    d = jnp.concatenate(
        [
            jnp.concatenate([r3[h * 128 : h * 128 + 128, l * 64 : l * 64 + 64] for h in range(4)], axis=1)
            for l in range(2)
        ],
        axis=0,
    )
    return jnp.concatenate([d, d], axis=0)


def inverse_xy(d, txi, tyi):
    g = mm(jnp.concatenate(txi, axis=0), d).astype(BF)
    g = [jnp.concatenate([g[k * 64 : k * 64 + 32], g[k * 64 + 32 : k * 64 + 64]], axis=1) for k in range(len(txi))]
    o = mm(jnp.concatenate(g, axis=0), tyi).astype(BF)
    return [
        [o[k * 32 : k * 32 + 32, h * 128 : h * 128 + 128].reshape(2, 4, 4, 128) for h in range(4)]
        for k in range(len(txi))
    ]


def inverse_z(r4, tzi):
    halves = [
        jnp.concatenate([r4[:, o].reshape(128, 128)[:, r * 64 : r * 64 + 64] for o in range(4)], axis=1)
        for r in range(2)
    ]
    res = mm(jnp.concatenate(halves, axis=0), tzi, TN)
    return jnp.transpose(res.reshape(4, 8, 8, 512), (1, 0, 2, 3)).reshape(256, 512)


def gelu(v):
    return 0.5 * v * (1.0 + lax.erf(v * (0.5**0.5)))


def far_first(sizes):
    steps = [()]
    for n in sizes:
        steps = [s + (k,) for s in steps for k in range(n)]
    steps = [s + (c,) for s in steps for c in range(2)]
    steps.sort(key=lambda s: (-sum(min(k, n - k) for k, n in zip(s, sizes)), -s[-1]))
    return steps[:-1]


def kernel(
    x_hbm, diff_hbm, w_hbm, point_hbm, off_hbm, tz_hbm, tx_hbm, ty_hbm, txi_hbm, tyi_hbm, tzi_hbm,
    out_ref,
    x_v, diff_v, w_v, wide_v, spread_v, order_v, point_ref, off_ref, tz_v, tx_v, ty_v, txi_v, tyi_v, tzi_v, pre_v,
    s1, r1, s2, r2, s3, r3, s4, r4, load_sem, send_sem, recv_sem,
):
    g, h = lax.axis_index("gx"), lax.axis_index("gy")
    plane, zz = g // 4, g % 4
    kz = plane * 4 + h
    yy, xc, core = g // 8, (plane % 2) * 2 + h // 2, h % 2
    ys = [lax.rem(yy + k, 4) for k in range(4)]
    zs = [lax.rem(zz + k, 4) for k in range(4)]
    xs = [lax.rem(xc + k, 4) for k in range(4)]
    xhs = [xs[b] // 2 for b in range(4)]
    ups = [[ys[a] * 8 + xhs[b] * 4 for b in range(4)] for a in range(4)]
    gys = [[xs[b] % 2 * 2 + c for c in (core, 1 - core)] for b in range(4)]
    everyone = [(ups[a][b] + zs[c], gys[b][d]) for a, b, c, d in far_first((4, 4, 4))]
    planar = [(ups[a][b], gys[b][d]) for a, b, d in far_first((4, 4))]

    barrier = pltpu.get_barrier_semaphore()
    for peer in everyone:
        pl.semaphore_signal(barrier, inc=1, device_id=peer, device_id_type=MESH)

    loads = [
        (x_hbm, x_v), (tz_hbm, tz_v), (diff_hbm, diff_v), (point_hbm, point_ref), (off_hbm, off_ref), (tx_hbm.at[zz], tx_v), (ty_hbm, ty_v),
        (w_hbm, w_v), (txi_hbm.at[zz], txi_v), (tyi_hbm, tyi_v), (tzi_hbm, tzi_v),
    ]
    loads = [pltpu.make_async_copy(a, b, load_sem.at[k]) for k, (a, b) in enumerate(loads)]
    for c in loads:
        c.start()
    loads[0].wait()
    loads[1].wait()
    xx = cells_by_x(x_v[...]).astype(BF)
    for q, block in enumerate(forward_z(xx, tz_v[...])):
        s1[:, q] = block
    for c in loads[2:5]:
        c.wait()
    diff = diff_v[...].astype(F32)
    pre_v[...] = before_gelu(None, xx, diff, point_ref[...], lambda o: off_ref[o])
    for c in loads[5:]:
        c.wait()
    pl.semaphore_wait(barrier, 127)

    def send(src, dst, phase, peer):
        pltpu.make_async_remote_copy(
            src, dst, send_sem.at[phase], recv_sem.at[phase], device_id=peer, device_id_type=MESH
        ).start()

    def wait(ref, sem):
        pltpu.make_async_copy(ref, ref, sem).wait()

    slot = h * 8 + plane
    for up, gy in planar:
        send(s1.at[up + gy], r1.at[slot], 0, (up + zz, gy))
    r1[slot] = s1[kz]
    spread_v[...] = spread_table()
    order_v[...] = order_table()
    for m in range(16):
        wide_v[m] = w_v[m].astype(F32)
    wait(r1.at[pl.ds(0, 31)], recv_sem.at[0])

    e = forward_y(r1[...], ty_v[...])
    slot = zz * 32 + kz
    for near in ((2, 1), (3, 0)):
        for k, blocks in zip(near, forward_x(e, [tx_v[ys[k]] for k in near])):
            for j, block in enumerate(blocks):
                s2[j, ys[k]] = block
        for a, b, c, d in far_first((4, 4, 4)):
            if a in near:
                up, gy = xhs[b] * 4 + zs[c], gys[b][d]
                send(s2.at[gy, ys[a], up], r2.at[slot], 1, (ys[a] * 8 + up, gy))
    r2[slot] = s2[h, yy, g % 8]
    wait(r2.at[pl.ds(0, 127)], recv_sem.at[1])

    s3[...] = mix_modes(own_modes(r2[...], spread_v[...]), lambda m: wide_v[m], order_v[...])
    slot = h * 32 + g
    for a, b, c, d in far_first((4, 4, 4)):
        up, gy = ups[a][b], gys[b][d]
        send(s3.at[up + gy], r3.at[slot], 2, (up + zs[c], gy))
    r3[slot] = s3[kz]
    wait(r3.at[pl.ds(0, 127)], recv_sem.at[2])

    modes = modes_by_kx(r3[...])
    for near in ((2, 1), (3, 0)):
        for k, blocks in zip(near, inverse_xy(modes, [txi_v[ys[k]] for k in near], tyi_v[...])):
            for j, block in enumerate(blocks):
                s4[ys[k], :, j] = block
        for a, b, d in far_first((4, 4)):
            if a in near:
                send(s4.at[ys[a], xhs[b], gys[b][d]], r4.at[kz], 3, (ups[a][b] + zz, gys[b][d]))
    r4[kz] = s4[yy, plane % 2, h]
    wait(r1.at[pl.ds(0, 31)], recv_sem.at[3])

    act = gelu(pre_v[...] + inverse_z(r4[...], tzi_v[...]))
    act = jnp.stack([act[:, k * 128 : k * 128 + 128].reshape(32, 8, 128) for k in range(4)], axis=1)
    out_ref[...] = act.reshape(1024, 128).astype(BF)

    wait(s1.at[pl.ds(0, 31)], send_sem.at[0])
    wait(r2.at[pl.ds(0, 127)], send_sem.at[1])
    wait(r2.at[pl.ds(0, 127)], send_sem.at[2])
    wait(s1.at[pl.ds(0, 31)], send_sem.at[3])


def on_device(inputs, diffusion, spectral, pointwise, offsets):
    hbm = pl.BlockSpec(memory_space=pltpu.HBM)
    vmem = pl.BlockSpec(memory_space=pltpu.VMEM)
    v = pltpu.VMEM
    args = [inputs.reshape(1024, 128), diffusion, spectral.reshape(16, 32, 1024), pointwise, offsets, *tables()]
    out = pl.pallas_call(
        kernel,
        out_shape=jax.ShapeDtypeStruct((1024, 128), BF),
        in_specs=[hbm] * 11,
        out_specs=vmem,
        scratch_shapes=[
            v((1024, 128), BF), v((4, 8, 128), BF), v((16, 32, 1024), BF), v((16, 32, 1024), F32), v((256, 512), BF), v((128, 128), BF), v((32, 32), BF), pltpu.SMEM((32,), F32),
            v((256, 512), BF), v((4, 64, 768), BF), v((512, 512), BF),
            v((4, 64, 512), BF), v((512, 512), BF), v((256, 512), BF), v((256, 512), F32),
            v((32, 4, 4, 128), BF), v((32, 4, 4, 128), BF),
            v((4, 4, 8, 4, 128), BF), v((128, 4, 128), BF),
            v((32, 4, 128), BF), v((128, 4, 128), BF),
            v((4, 2, 4, 4, 4, 128), BF), v((32, 4, 4, 128), BF),
            pltpu.SemaphoreType.DMA((11,)), pltpu.SemaphoreType.DMA((4,)), pltpu.SemaphoreType.DMA((4,)),
        ],
        compiler_params=pltpu.CompilerParams(
            collective_id=0, has_side_effects=True, vmem_limit_bytes=40 << 20
        ),
    )(*[pltpu.with_memory_space_constraint(a, pltpu.HBM) for a in args])
    return out.reshape(32, 4, 8, 128)


def solution(mesh):
    return jax.shard_map(
        on_device,
        mesh=mesh,
        in_specs=(P(None, "gx", "gy", None), P("gx", "gy", None), P("gx", "gy", None, None, None), P(), P()),
        out_specs=P(None, "gx", "gy", None),
        check_vma=False,
    )
```

```python
import functools

import jax
import jax.numpy as jnp
import ml_dtypes
import numpy as np
from jax import lax
from jax.experimental import pallas as pl
from jax.experimental.pallas import tpu as pltpu
from jax.sharding import PartitionSpec as P

MESH = pl.DeviceIdType.MESH
BF = jnp.bfloat16
F32 = jnp.float32

NT = (((1,), (1,)), ((), ()))
TN = (((0,), (0,)), ((), ()))
NN = (((1,), (0,)), ((), ()))


def mm(a, b, dims=NN):
    return lax.dot_general(a, b, dims, preferred_element_type=F32)


def freq(n):
    j = np.arange(n)
    return np.where(j < n // 2, j, j - n)


def turn(a, b, n):
    return 2.0 * np.pi / n * ((a * b) % n)


def parts(z):
    return np.stack([z.real, z.imag])


def two_parts(t, axis, order):
    high = np.asarray(t, np.float32).astype(ml_dtypes.bfloat16).astype(np.float64)
    return np.concatenate([(high, t - high)[k] for k in order], axis=axis)


def tables():
    eye4, eye8 = np.eye(4), np.eye(8)
    z, kz = np.arange(128), np.arange(32)
    a = parts(np.exp(-1j * turn(kz[:, None], z[None, :], 128)))
    tz = np.einsum("rkz,xw->rkxwz", a, eye4).reshape(256, 512)
    unit = np.array([1.0, 1j])
    y = np.arange(32).reshape(4, 8)
    ky = freq(16).reshape(4, 4)
    ph = turn(y[:, :, None, None], ky[None, None], 32)
    co = np.einsum("hyHk,s,r->hyHksr", np.exp(-1j * ph), np.conj(unit), unit)
    ty = np.einsum("qhyHksr,cd->hrcysHkqd", parts(co), eye8).reshape(512, 512)
    x = 4 * (4 * np.arange(8)[None, :, None] + np.arange(4)[:, None, None]) + np.arange(4)
    kx = np.transpose(freq(64).reshape(4, 8, 2), (0, 2, 1))
    th = turn(kx[None, None, None], x[:, :, :, None, None, None], 128)
    cs = np.stack([np.cos(th), np.sin(th)])
    tx = np.einsum("sZYxylg,cd->ZylgcsYdx", cs, eye4).reshape(4, 4, 64, 256)
    cs = cs.reshape(2, 4, 4, 2, 4, 4, 2, 8)
    txi = np.einsum("sZYhxylg,cd->ZYshcxlygd", cs, eye4).reshape(4, 4, 64, 256)
    co = np.einsum("HyhK,s,r->HyhKsr", np.exp(1j * ph), unit, unit)
    tyi = np.einsum("qHyhKsr,bd->shbKrHqdy", parts(co), eye8).reshape(512, 512)
    b = np.exp(1j * turn(kz[:, None], z[None, :], 128)) * 2.0**-7.5
    tzi = np.einsum("rkz,xw->rkxwz", np.stack([b.real, -b.imag]), eye4).reshape(256, 512)
    tx, txi = two_parts(tx, 3, (0, 1, 0)), two_parts(txi, 3, (0, 1))
    return [jnp.asarray(np.asarray(t, np.float32).astype(ml_dtypes.bfloat16)) for t in (tz, tx, ty, txi, tyi, tzi)]


def iota(shape, dim):
    return lax.broadcasted_iota(jnp.int32, shape, dim)


def one_hot(cond):
    return jnp.where(cond, 1.0, 0.0).astype(BF)


def cells_by_x(x):
    wide = x.astype(F32).reshape(32, 4, 8, 128)
    return jnp.concatenate([wide[:, k].reshape(256, 128) for k in range(4)], axis=1)


def forward_z(xx, tz):
    out = mm(tz, xx, NT)
    res = []
    for q in range(4):
        lanes = slice(q * 64, q * 64 + 64)
        both = jnp.concatenate([out[:128, lanes], out[128:, lanes]], axis=1)
        res.append(both.astype(BF).reshape(32, 4, 128))
    return res


def before_gelu(wide, xx, diff, point, offset):
    rep = one_hot(iota((256, 32), 0) // 8 == iota((256, 32), 1))
    spread = mm(mm(rep, point).astype(BF), rep, NT)
    same_y = iota((256, 256), 0) % 8 == iota((256, 256), 1) % 8
    kron = jnp.where(same_y, spread, 0.0).astype(BF)
    mix = mm(kron, xx)
    gap = iota((128, 128), 0) - iota((128, 128), 1)
    sten = jnp.where(gap == 0, -2.0, jnp.where((gap == 1) | (gap == -1), 1.0, 0.0)).astype(BF)
    cols = []
    for k in range(4):
        lanes = slice(k * 128, k * 128 + 128)
        curv = mm(xx[:, lanes], sten).reshape(32, 8, 128)
        cols.append((curv * diff[k][None]).reshape(256, 128))
    shift = jnp.concatenate([jnp.full((8, 512), offset(o), F32) for o in range(32)], axis=0)
    return mix + jnp.concatenate(cols, axis=1) + shift


def forward_y(r1, ty):
    r1 = r1.reshape(512, 128)
    d = jnp.concatenate([r1[h * 128 : h * 128 + 128] for h in range(4)], axis=1)
    e = mm(d, ty)
    e = jnp.concatenate([e[:, :256], e[:, 256:]], axis=0)
    high = e.astype(BF)
    return jnp.concatenate([high, high, (e - high.astype(F32)).astype(BF)], axis=0)


def forward_x(e, tx):
    o = mm(jnp.concatenate(tx, axis=0), e)
    res = []
    for k in range(len(tx)):
        lo, hi = o[k * 64 : k * 64 + 32], o[k * 64 + 32 : k * 64 + 64]
        both = [jnp.concatenate([lo[:, h * 64 : h * 64 + 64], hi[:, h * 64 : h * 64 + 64]], axis=1) for h in range(4)]
        res.append([b.astype(BF).reshape(8, 4, 128) for b in both])
    return res


def spread_table():
    row, col = iota((256, 512), 0) % 128, iota((256, 512), 1)
    return one_hot((row % 4 == col // 128) & (row // 4 == col % 32))


def order_table():
    row, col = iota((128, 128), 0), iota((128, 128), 1)
    return one_hot((row % 4 == col // 32) & (row // 4 == col % 32))


def own_modes(r2, spread):
    r2 = r2.reshape(512, 128).astype(F32)
    u = r2[:128] + r2[128:256] + r2[256:384] + r2[384:]
    hi = u.astype(BF)
    lo = (u - hi.astype(F32)).astype(BF)
    return mm(jnp.concatenate([hi, lo], axis=0), spread, TN) * (2.0**-9.5)


def sum_rows(acc):
    row = iota(acc[0].shape, 0)
    half = row < 4
    four = [
        jnp.where(half, acc[k], acc[k + 4]) + pltpu.roll(jnp.where(half, acc[k + 4], acc[k]), 4, 0)
        for k in range(4)
    ]

    def join(a, b, k):
        return jnp.where(row % (2 * k) < k, a + pltpu.roll(a, 8 - k, 0), b + pltpu.roll(b, k, 0))

    return join(join(four[0], four[2], 2), join(four[1], four[3], 2), 1)


def mix_modes(u, w, order):
    blocks = []
    for l in range(2):
        acc = []
        for j in range(4 * l, 4 * l + 4):
            wr, wi = w(2 * j), w(2 * j + 1)
            re = im = None
            for q in range(4):
                ur = jnp.concatenate([u[16 * j : 16 * j + 8, q * 128 : q * 128 + 128]] * 8, axis=1)
                ui = jnp.concatenate([u[16 * j + 8 : 16 * j + 16, q * 128 : q * 128 + 128]] * 8, axis=1)
                r, i = wr[q * 8 : q * 8 + 8], wi[q * 8 : q * 8 + 8]
                a, b = r * ur - i * ui, r * ui + i * ur
                re, im = (a, b) if re is None else (re + a, im + b)
            acc += [re, im]
        y = sum_rows(acc)
        blocks += [y[:, b * 128 : b * 128 + 128] for b in range(8)]
    a = jnp.concatenate(blocks, axis=0).astype(BF)
    return mm(order, a, NT).astype(BF).reshape(32, 4, 128)


def modes_by_kx(r3):
    r3 = r3.reshape(512, 128)
    d = jnp.concatenate(
        [
            jnp.concatenate([r3[h * 128 : h * 128 + 128, l * 64 : l * 64 + 64] for h in range(4)], axis=1)
            for l in range(2)
        ],
        axis=0,
    )
    return jnp.concatenate([d, d], axis=0)


def inverse_xy(d, txi, tyi):
    g = mm(jnp.concatenate(txi, axis=0), d).astype(BF)
    g = [jnp.concatenate([g[k * 64 : k * 64 + 32], g[k * 64 + 32 : k * 64 + 64]], axis=1) for k in range(len(txi))]
    o = mm(jnp.concatenate(g, axis=0), tyi).astype(BF)
    return [
        [o[k * 32 : k * 32 + 32, h * 128 : h * 128 + 128].reshape(2, 4, 4, 128) for h in range(4)]
        for k in range(len(txi))
    ]


def inverse_z(r4, tzi):
    halves = [
        jnp.concatenate([r4[:, o].reshape(128, 128)[:, r * 64 : r * 64 + 64] for o in range(4)], axis=1)
        for r in range(2)
    ]
    res = mm(jnp.concatenate(halves, axis=0), tzi, TN)
    return jnp.transpose(res.reshape(4, 8, 8, 512), (1, 0, 2, 3)).reshape(256, 512)


def gelu(v):
    return 0.5 * v * (1.0 + lax.erf(v * (0.5**0.5)))


def far_first(sizes):
    steps = [()]
    for n in sizes:
        steps = [s + (k,) for s in steps for k in range(n)]
    steps = [s + (c,) for s in steps for c in range(2)]
    steps.sort(key=lambda s: (-sum(min(k, n - k) for k, n in zip(s, sizes)), -s[-1]))
    return steps[:-1]


def kernel(
    x_hbm, diff_hbm, w_hbm, point_hbm, off_hbm, tz_hbm, tx_hbm, ty_hbm, txi_hbm, tyi_hbm, tzi_hbm,
    out_ref,
    x_v, diff_v, w_v, wide_v, spread_v, order_v, point_ref, off_ref, tz_v, tx_v, ty_v, txi_v, tyi_v, tzi_v, pre_v,
    s1, r1, s2, r2, s3, r3, s4, r4, load_sem, send_sem, recv_sem,
):
    g, h = lax.axis_index("gx"), lax.axis_index("gy")
    plane, zz = g // 4, g % 4
    kz = plane * 4 + h
    yy, xc, core = g // 8, (plane % 2) * 2 + h // 2, h % 2
    ys = [lax.rem(yy + k, 4) for k in range(4)]
    zs = [lax.rem(zz + k, 4) for k in range(4)]
    xs = [lax.rem(xc + k, 4) for k in range(4)]
    xhs = [xs[b] // 2 for b in range(4)]
    ups = [[ys[a] * 8 + xhs[b] * 4 for b in range(4)] for a in range(4)]
    gys = [[xs[b] % 2 * 2 + c for c in (core, 1 - core)] for b in range(4)]
    everyone = [(ups[a][b] + zs[c], gys[b][d]) for a, b, c, d in far_first((4, 4, 4))]
    planar = [(ups[a][b], gys[b][d]) for a, b, d in far_first((4, 4))]

    barrier = pltpu.get_barrier_semaphore()
    for peer in everyone:
        pl.semaphore_signal(barrier, inc=1, device_id=peer, device_id_type=MESH)

    loads = [
        (x_hbm, x_v), (tz_hbm, tz_v), (diff_hbm, diff_v), (point_hbm, point_ref), (off_hbm, off_ref), (tx_hbm.at[zz], tx_v), (ty_hbm, ty_v),
        (w_hbm, w_v), (txi_hbm.at[zz], txi_v), (tyi_hbm, tyi_v), (tzi_hbm, tzi_v),
    ]
    loads = [pltpu.make_async_copy(a, b, load_sem.at[k]) for k, (a, b) in enumerate(loads)]
    for c in loads:
        c.start()
    loads[0].wait()
    loads[1].wait()
    xx = cells_by_x(x_v[...]).astype(BF)
    for q, block in enumerate(forward_z(xx, tz_v[...])):
        s1[:, q] = block
    for c in loads[2:5]:
        c.wait()
    diff = diff_v[...].astype(F32)
    pre_v[...] = before_gelu(None, xx, diff, point_ref[...], lambda o: off_ref[o])
    for c in loads[5:]:
        c.wait()
    pl.semaphore_wait(barrier, 127)

    def send(src, dst, phase, peer):
        pltpu.make_async_remote_copy(
            src, dst, send_sem.at[phase], recv_sem.at[phase], device_id=peer, device_id_type=MESH
        ).start()

    def wait(ref, sem):
        pltpu.make_async_copy(ref, ref, sem).wait()

    slot = h * 8 + plane
    for up, gy in planar:
        send(s1.at[up + gy], r1.at[slot], 0, (up + zz, gy))
    r1[slot] = s1[kz]
    spread_v[...] = spread_table()
    order_v[...] = order_table()
    for m in range(16):
        wide_v[m] = w_v[m].astype(F32)
    wait(r1.at[pl.ds(0, 31)], recv_sem.at[0])

    e = forward_y(r1[...], ty_v[...])
    slot = zz * 32 + kz
    for near in ((2, 1), (3, 0)):
        for k, blocks in zip(near, forward_x(e, [tx_v[ys[k]] for k in near])):
            for j, block in enumerate(blocks):
                s2[j, ys[k]] = block
        for a, b, c, d in far_first((4, 4, 4)):
            if a in near:
                up, gy = xhs[b] * 4 + zs[c], gys[b][d]
                send(s2.at[gy, ys[a], up], r2.at[slot], 1, (ys[a] * 8 + up, gy))
    r2[slot] = s2[h, yy, g % 8]
    wait(r2.at[pl.ds(0, 127)], recv_sem.at[1])

    s3[...] = mix_modes(own_modes(r2[...], spread_v[...]), lambda m: wide_v[m], order_v[...])
    slot = h * 32 + g
    for a, b, c, d in far_first((4, 4, 4)):
        up, gy = ups[a][b], gys[b][d]
        send(s3.at[up + gy], r3.at[slot], 2, (up + zs[c], gy))
    r3[slot] = s3[kz]
    wait(r3.at[pl.ds(0, 127)], recv_sem.at[2])

    modes = modes_by_kx(r3[...])
    for k, blocks in enumerate(inverse_xy(modes, [txi_v[k] for k in range(4)], tyi_v[...])):
        for j, block in enumerate(blocks):
            s4[k, :, j] = block
    places = [(p, q, c) for p in range(4) for q in range(4) for c in range(2)]
    for yd, xd, cd in sorted(places, key=lambda t: (t[0] + t[1], t)):

        @pl.when((yy != yd) | (xc != xd) | (core != cd))
        def _(yd=yd, xh=xd // 2, gy=xd % 2 * 2 + cd):
            send(s4.at[yd, xh, gy], r4.at[kz], 3, (yd * 8 + xh * 4 + zz, gy))
    r4[kz] = s4[yy, plane % 2, h]
    wait(r1.at[pl.ds(0, 31)], recv_sem.at[3])

    act = gelu(pre_v[...] + inverse_z(r4[...], tzi_v[...]))
    act = jnp.stack([act[:, k * 128 : k * 128 + 128].reshape(32, 8, 128) for k in range(4)], axis=1)
    out_ref[...] = act.reshape(1024, 128).astype(BF)

    wait(s1.at[pl.ds(0, 31)], send_sem.at[0])
    wait(r2.at[pl.ds(0, 127)], send_sem.at[1])
    wait(r2.at[pl.ds(0, 127)], send_sem.at[2])
    wait(s1.at[pl.ds(0, 31)], send_sem.at[3])


def on_device(inputs, diffusion, spectral, pointwise, offsets):
    hbm = pl.BlockSpec(memory_space=pltpu.HBM)
    vmem = pl.BlockSpec(memory_space=pltpu.VMEM)
    v = pltpu.VMEM
    args = [inputs.reshape(1024, 128), diffusion, spectral.reshape(16, 32, 1024), pointwise, offsets, *tables()]
    out = pl.pallas_call(
        kernel,
        out_shape=jax.ShapeDtypeStruct((1024, 128), BF),
        in_specs=[hbm] * 11,
        out_specs=vmem,
        scratch_shapes=[
            v((1024, 128), BF), v((4, 8, 128), BF), v((16, 32, 1024), BF), v((16, 32, 1024), F32), v((256, 512), BF), v((128, 128), BF), v((32, 32), BF), pltpu.SMEM((32,), F32),
            v((256, 512), BF), v((4, 64, 768), BF), v((512, 512), BF),
            v((4, 64, 512), BF), v((512, 512), BF), v((256, 512), BF), v((256, 512), F32),
            v((32, 4, 4, 128), BF), v((32, 4, 4, 128), BF),
            v((4, 4, 8, 4, 128), BF), v((128, 4, 128), BF),
            v((32, 4, 128), BF), v((128, 4, 128), BF),
            v((4, 2, 4, 4, 4, 128), BF), v((32, 4, 4, 128), BF),
            pltpu.SemaphoreType.DMA((11,)), pltpu.SemaphoreType.DMA((4,)), pltpu.SemaphoreType.DMA((4,)),
        ],
        compiler_params=pltpu.CompilerParams(
            collective_id=0, has_side_effects=True, vmem_limit_bytes=40 << 20
        ),
    )(*[pltpu.with_memory_space_constraint(a, pltpu.HBM) for a in args])
    return out.reshape(32, 4, 8, 128)


def solution(mesh):
    return jax.shard_map(
        on_device,
        mesh=mesh,
        in_specs=(P(None, "gx", "gy", None), P("gx", "gy", None), P("gx", "gy", None, None, None), P(), P()),
        out_specs=P(None, "gx", "gy", None),
        check_vma=False,
    )
```
